32 devices in a mesh: runs: 2 (over y), grp: 4 (over x, core), mem: 4 (over z).
Axes of the slice: x: 2, y: 2, z: 4, core: 2. Of those that a mesh axis runs over, the one named last changes fastest.
Arguments:
- coords: float32 [256, 3, 512], P(('runs', 'grp', 'mem')), parts along dimension 0, may hold values from 0 to 128, as said below
- noise: float32 [256, 512], P(('runs', 'grp', 'mem')), parts along dimension 0, may hold values from 0.2 to 1
- right_side: float32 [256, 512], P(('runs', 'grp', 'mem')), parts along dimension 0, may hold values from -11 to 11
- tiles: int32 [256, 4, 2], P(('runs', 'grp', 'mem')), parts along dimension 0, may hold values from 0 to 127, as said below
- tile_count: int32 [256], P(('runs', 'grp', 'mem')), parts along dimension 0, may hold values from 1 to 4
Outputs:
- solution: float32 [256, 512], P(('runs', 'grp', 'mem')), parts along dimension 0
- residual: float32 [256, 512], P(('runs', 'grp', 'mem')), parts along dimension 0
The draws below stay inside these ranges and needn't reach their ends.
There are 2 independent parts, one for each index of `runs`. The reference program is written for one: setup_inputs(seed, part) draws one part's arguments, and reference() takes and returns one part's arrays. A program takes and returns all parts, laid end to end along the dimension named above; each array names one. Nothing has to cross between parts.
Inputs may be any that keep to these rules, and one draw needn't show every extreme that they name: `tiles`: slot k < tile_count[r] of block row r holds (r, r + k); the remaining slots hold (r, r). Every block c >= r whose kernel tile with r is nonzero is listed. `coords`: the time coordinate of block b lies in [k, k + 1) for an integer time cell k of the block; every block lies wholly in one time cell, cells are nondecreasing along the blocks, and each cell holds 1 to 2 consecutive blocks.
All inputs are finite; a program needn't handle non-finite values.
Results may differ from the reference program's by a relative error of at most 0.0003.
Values sent between devices are 32-bit elements; how exact they have to be, the bound alone decides.
No kernel may reach another device: no remote copies, remote signals or barrier semaphores. Data moves between devices by JAX's collectives and lax.ppermute only.
A program may use at most 64 MiB of HBM per device.

```python
import math
import jax
import jax.numpy as jnp
from jax import lax

B = 512
MOST = 2
TMAX = 4
ITERS = 2
NB = 128


def cell_of_block(key):
    sizes = jax.random.randint(jax.random.fold_in(key, 11), (NB,), 1, MOST + 1)
    paired = jax.random.randint(jax.random.fold_in(key, 12), (), 0, NB // MOST - 1)
    blocks = jnp.arange(NB, dtype=jnp.int32)
    sizes = jnp.where((blocks == paired) | (blocks == paired + 1), MOST, sizes)
    starts = jnp.cumsum(sizes) - sizes
    return jnp.sum((starts[None, :] <= blocks[:, None]).astype(jnp.int32), axis=1) - 1


def tile_pairs(key):
    cell = cell_of_block(key)
    rows = jnp.arange(NB, dtype=jnp.int32)[:, None]
    columns = rows + jnp.arange(TMAX, dtype=jnp.int32)[None, :]
    clipped = jnp.minimum(columns, NB - 1)
    valid = (columns < NB) & (cell[clipped] <= cell[rows[:, 0]][:, None] + 1)
    listed = jnp.where(valid, columns, rows)
    pairs = jnp.stack([jnp.broadcast_to(rows, listed.shape), listed], axis=-1)
    return (pairs.astype(jnp.int32), jnp.sum(valid.astype(jnp.int32), axis=1))


def draw_tiles(key, part):
    pairs, counts = tile_pairs(key)
    return pairs


def draw_tile_count(key, part):
    pairs, counts = tile_pairs(key)
    return counts


def draw_coords(key, part):
    cell = cell_of_block(key).astype(jnp.float32)
    key = jax.random.fold_in(key, 3)
    first, second = jax.random.split(key)
    place = jax.random.uniform(first, (NB, 2, B), jnp.float32) * 3.0
    when = cell[:, None] + jax.random.uniform(second, (NB, B), jnp.float32) * 0.999
    return jnp.concatenate([place, when[:, None, :]], axis=1)


def draw_right_side(key, part):
    key = jax.random.fold_in(key, 5)
    first, second = jax.random.split(key)
    rise = (0.6 + 1.2 * jnp.arange(NB, dtype=jnp.float32) / NB)[:, None]
    value = jnp.clip(jax.random.normal(first, (NB, B), jnp.float32), -4.0, 4.0)
    spread = jnp.exp(jax.random.uniform(second, (NB, B), jnp.float32, -0.35, 0.35))
    return value * rise * spread


def block_scale(key, dims, shards, smallest, top_value):
    gain, own = 1.0, jax.random.fold_in(key, 6)
    for dim, shards_of in shards:
        heights = jnp.exp(jax.random.uniform(jax.random.fold_in(own, dim), (shards_of,), jnp.float32, smallest / len(shards), top_value / len(shards)))
        gain = gain * jnp.repeat(heights, dims[dim] // shards_of).reshape([-1 if axis == dim else 1 for axis in range(len(dims))])
    return gain


def setup_inputs(seed: int = 0, part: int = 0) -> dict:
    splits = jax.random.split(jax.random.key(seed), 6)
    own_keys = jax.random.split(jax.random.fold_in(splits[5], part), 6)
    return {
        "coords": draw_coords(jax.random.fold_in(jax.random.fold_in(splits[5], part), 71), part),
        "noise": jnp.clip(jnp.exp(math.log(1.0) - 1.609438 * jax.random.uniform(own_keys[1], (NB, B), jnp.float32) ** block_scale(own_keys[1], (NB, B), ((0, 16),), -0.2, 0.2)), 0.2, 1.0),
        "right_side": draw_right_side(jax.random.fold_in(jax.random.fold_in(splits[5], part), 71), part),
        "tiles": draw_tiles(jax.random.fold_in(jax.random.fold_in(splits[5], part), 71), part),
        "tile_count": draw_tile_count(jax.random.fold_in(jax.random.fold_in(splits[5], part), 71), part),
    }


AMPLITUDE = 0.2
PRECISE = lax.Precision.HIGHEST

def wendland(distance):
    remain = jnp.maximum(1.0 - distance, 0.0)
    return remain ** 4 * (4.0 * distance + 1.0)

def tile_kernel(left, right):
    across_x = left[0][:, None] - right[0][None, :]
    across_y = left[1][:, None] - right[1][None, :]
    across_t = left[2][:, None] - right[2][None, :]
    spatial = jnp.sqrt(across_x * across_x + across_y * across_y)
    return AMPLITUDE * wendland(spatial) * wendland(jnp.abs(across_t))

def apply_kernel(vector, coords, tiles, tile_count):

    def row_step(total, block_row):
        own_vector = vector[block_row]
        own_coords = coords[block_row]

        def tile_step(slot, partial_value):
            block_col = tiles[block_row, slot, 1]
            kernel_tile = tile_kernel(own_coords, coords[block_col])
            partial_value = partial_value.at[block_row].add(jnp.dot(kernel_tile, vector[block_col], precision=PRECISE))
            mirror = jnp.where(block_col != block_row, 1.0, 0.0) * jnp.dot(own_vector, kernel_tile, precision=PRECISE)
            return partial_value.at[block_col].add(mirror)
        total = lax.fori_loop(0, tile_count[block_row], tile_step, total)
        return (total, None)
    total, unused = lax.scan(row_step, jnp.zeros_like(vector), jnp.arange(NB, dtype=jnp.int32))
    return total

def reference(coords, noise, right_side, tiles, tile_count):
    solution = jnp.zeros_like(right_side)
    residual = right_side
    direction = right_side
    norm_now = jnp.sum(residual * residual)
    for step in range(ITERS):
        image = noise * direction + apply_kernel(direction, coords, tiles, tile_count)
        alpha = norm_now / jnp.sum(direction * image)
        solution = solution + alpha * direction
        residual = residual - alpha * image
        norm_next = jnp.sum(residual * residual)
        direction = residual + norm_next / norm_now * direction
        norm_now = norm_next
    return (solution, residual)
```

```python
import functools

import jax
import jax.numpy as jnp
from jax import lax
from jax.experimental import pallas as pl
from jax.experimental.pallas import tpu as pltpu
from jax.sharding import PartitionSpec as P

SCALE = 0.2 * 16.0
TINY = 1e-30
LANES = 128
SUBLANES = 8
UNROLL = 16
AXES = ("grp", "mem")
MIB = 1 << 20
X, Y, T, V, COUNT = range(5)

VMEM = pl.BlockSpec(memory_space=pltpu.VMEM)
SMEM = pl.BlockSpec(memory_space=pltpu.SMEM)


def resident(*arrays):
    return [pltpu.with_memory_space_constraint(a, pltpu.VMEM) for a in arrays]


def call(kernel, out_shape, operands, specs, scratch=(), limit=12):
    return pl.pallas_call(
        kernel,
        out_shape=out_shape,
        in_specs=specs,
        out_specs=jax.tree.map(lambda _: VMEM, out_shape),
        scratch_shapes=list(scratch),
        compiler_params=pltpu.CompilerParams(vmem_limit_bytes=limit * MIB),
    )(*operands)


def shape(*dims):
    return jax.ShapeDtypeStruct(dims, jnp.float32)


def vmem(*dims):
    return pltpu.VMEM(dims, jnp.float32)


def entries(xi, yi, ti, xj, yj, tj, mode):
    dx = xi - xj
    dy = yi - yj
    u = jnp.maximum(dx * dx + dy * dy, TINY)
    s = u * lax.rsqrt(u)
    a = jnp.maximum(1.0 - s, 0.0)
    if mode == "same":
        d = jnp.abs(ti - tj)
        b = 1.0 - d
        f = d + 0.25
    elif mode == "any":
        d = jnp.abs(ti - tj)
        b = jnp.maximum(1.0 - d, 0.0)
        f = d + 0.25
    else:
        b = jnp.maximum(ti - tj, 0.0) if mode == "next" else jnp.maximum(tj - ti, 0.0)
        f = 1.25 - b
    p = a * b
    p = p * p
    return (p * p) * ((s + 0.25) * f)


def spread(row):
    return jnp.broadcast_to(row, (SUBLANES, row.shape[-1]))


def tile(make, load, rows_of, width, sum_ref, col_add, chunks_of, unroll=UNROLL):
    chunks = width // LANES

    def band(lo, hi, used, single):
        def step(it, acc):
            acc = list(acc)
            for uu in range(unroll):
                at = pl.ds(pl.multiple_of((it * unroll + uu) * SUBLANES, SUBLANES), SUBLANES)
                row = rows_of(at)
                total = None
                for q, ch in enumerate(used):
                    m = make(row, at, ch)
                    w = m * load(ch)
                    total = w if total is None else total + w
                    if col_add is not None and ch != single:
                        acc[q] = acc[q] + m * row[V]
                sum_ref[at, :] += total
            return tuple(acc)

        zero = jnp.zeros((SUBLANES, LANES), jnp.float32)
        acc = lax.fori_loop(
            lo // (SUBLANES * unroll), hi // (SUBLANES * unroll), step, tuple(zero for _ in used)
        )
        if col_add is not None:
            for q, ch in enumerate(used):
                if ch != single:
                    col_add(ch, acc[q])

    if chunks_of == "upper":
        for ri in range(chunks):
            band(ri * LANES, (ri + 1) * LANES, list(range(ri, chunks)), ri)
    else:
        band(0, width, list(range(chunks)), -1)


def cut(ch):
    return pl.ds(ch * LANES, LANES)


def new_tile(r, side, c, slot, mode, k_ref, cols, accl, accs, diag):
    width = side.shape[-1]
    chunks = width // LANES
    right = [[spread(side[c, q : q + 1, cut(ch)]) for ch in range(chunks)] for q in (X, Y, T, V)]
    if mode == "prev":
        right[T] = [t + 1.0 for t in right[T]]

    def rows_of(at):
        row = [cols[q, r, at, :] for q in (X, Y, T, V)]
        if mode == "next":
            row[T] = row[T] + 1.0
        return row

    def make(row, at, ch):
        m = entries(row[X], row[Y], row[T], right[X][ch], right[Y][ch], right[T][ch], mode)
        k_ref[slot, at, cut(ch)] = m
        return m

    col_add = None
    if accs is not None:

        def col_add(ch, value):
            accs[c, :, cut(ch)] += value

    tile(make, lambda ch: right[V][ch], rows_of, width, accl.at[r], col_add, "upper" if diag else "")


def old_tile(r, side, c, slot, k_ref, vcol, accl, accs, diag):
    width = side.shape[-1]
    chunks = width // LANES
    right = [spread(side[c, 0:1, cut(ch)]) for ch in range(chunks)]

    def rows_of(at):
        return {V: None if vcol is None else vcol[r, at, :]}

    col_add = None
    if accs is not None:

        def col_add(ch, value):
            accs[c, :, cut(ch)] += value

    tile(
        lambda row, at, ch: k_ref[slot, at, cut(ch)],
        lambda ch: right[ch],
        rows_of,
        width,
        accl.at[r],
        col_add,
        "upper" if diag else "",
    )


def inner_tiles(blocks, reach, count, body):
    base = 0
    for k in range(reach + 1):

        def step(r, _, k=k, base=base):
            pl.when(count[r] > k)(lambda: body(r, r + k, base + r, k))
            return 0

        lax.fori_loop(0, blocks - k, step, 0)
        base += blocks - k


def outer_tiles(blocks, reach, count, low_count, body):
    base = 0
    for k in range(1, reach + 1):

        def low(j, _, k=k, base=base):
            at = reach - k + j
            pl.when(low_count(at) > k)(lambda: body(j, 0, at, base + j, k))
            return 0

        def high(j, _, k=k, base=base):
            r = blocks - k + j
            pl.when(count[r] > k)(lambda: body(r, 1, j, base + k + j, k))
            return 0

        lax.fori_loop(0, k, low, 0)
        lax.fori_loop(0, k, high, 0)
        base += 2 * k


def pack_kernel(count, coords, vector, first, last, rows):
    blocks, _, width = rows.shape
    edge = first.shape[0]
    for b in range(blocks):
        rows[b, X : T + 1, :] = coords[b]
        rows[b, V : V + 1, :] = vector[b : b + 1, :]
        rows[b, COUNT:, :] = jnp.full((SUBLANES - COUNT, width), count[b].astype(jnp.float32))
    first[...] = rows[0:edge]
    last[...] = rows[blocks - edge :]


def inner_kernel(reach, count, packed, k_ref, cols, accl, accs, rows):
    blocks, _, width = packed.shape
    start = jnp.floor(packed[0, T : T + 1, 0:1])
    rows[...] = packed[...]
    for b in range(blocks):
        rows[b, T : T + 1, :] = packed[b, T : T + 1, :] - start

    def build(b, _):
        flat = rows[b].T
        for q in (X, Y, T, V):
            cols[q, b] = jnp.broadcast_to(flat[:, q : q + 1], (width, LANES))
        return 0

    lax.fori_loop(0, blocks, build, 0)
    accl[...] = jnp.zeros_like(accl)
    accs[...] = jnp.zeros_like(accs)

    def body(r, c, slot, k):
        mode = ("same", "any")[k] if k < 2 else "next"
        new_tile(r, rows, c, slot, mode, k_ref, cols, accl, accs, k == 0)

    inner_tiles(blocks, reach, count, body)


def outer_kernel(reach, count, low_in, high_in, packed, noise, cols, accl_in, accs, kx, image, first, last, low, high, accl):
    blocks = packed.shape[0]
    start = jnp.floor(packed[0, T : T + 1, 0:1])
    low[...] = low_in[...]
    high[...] = high_in[...]
    for b in range(reach):
        low[b, T : T + 1, :] = low_in[b, T : T + 1, :] - start
        high[b, T : T + 1, :] = high_in[b, T : T + 1, :] - start
    accl[...] = accl_in[...]

    def low_count(at):
        return jnp.max(low[at, COUNT : COUNT + 1, 0:LANES])

    def body(r, which, c, slot, k):
        mode = "any" if k == 1 else ("prev", "next")[which]
        new_tile(r, (low, high)[which], c, slot, mode, kx, cols, accl, None, False)

    outer_tiles(blocks, reach, count, low_count, body)
    summed = jnp.sum(accs[...], axis=1) + jnp.sum(accl[...], axis=-1)
    image[...] = noise[...] * packed[:, V, :] + SCALE * summed
    first[...] = image[0:reach, :]
    last[...] = image[blocks - reach :, :]


def again_kernel(reach, count, image, k_ref, accl, accs, rows, vcol):
    blocks, width = image.shape
    flat = image[...].T
    for b in range(blocks):
        rows[b, 0:1, :] = image[b : b + 1, :]
        vcol[b] = jnp.broadcast_to(flat[:, b : b + 1], (width, LANES))
    accl[...] = jnp.zeros_like(accl)
    accs[...] = jnp.zeros_like(accs)

    def body(r, c, slot, k):
        old_tile(r, rows, c, slot, k_ref, vcol, accl, accs, k == 0)

    inner_tiles(blocks, reach, count, body)


def dots(pairs):
    lane = lax.broadcasted_iota(jnp.int32, (1, LANES), 1)
    out = jnp.zeros((1, LANES), jnp.float32)
    for n, (a, b) in enumerate(pairs):
        total = jnp.sum(jnp.sum(a * b, axis=1, keepdims=True), axis=0, keepdims=True)
        out = jnp.where(lane == n, total, out)
    return out


def close_kernel(reach, count, low_in, high_in, low_packed, vector, noise, image, kx, accl_in, accs, again, sums, low, high, accl):
    blocks = image.shape[0]
    for b in range(reach):
        low[b, 0:1, :] = low_in[b : b + 1, :]
        high[b, 0:1, :] = high_in[b : b + 1, :]
    accl[...] = accl_in[...]

    def low_count(at):
        return jnp.max(low_packed[at, COUNT : COUNT + 1, 0:LANES])

    def body(r, which, c, slot, k):
        old_tile(r, (low, high)[which], c, slot, kx, None, accl, None, False)

    outer_tiles(blocks, reach, count, low_count, body)
    summed = jnp.sum(accs[...], axis=1) + jnp.sum(accl[...], axis=-1)
    q = image[...]
    p = noise[...] * q + SCALE * summed
    again[...] = p
    b = vector[...]
    sums[...] = jnp.broadcast_to(dots([(b, b), (b, q), (q, q), (b, p), (q, p)]), sums.shape)


def finish_kernel(sums, vector, image, again, solution, residual):
    total = jnp.sum(sums[...], axis=0, keepdims=True)
    bb, bq, qq, bp, qp = [total[:, n : n + 1] for n in range(5)]
    alpha = bb / bq
    rq = bq - alpha * qq
    rr = (bb - alpha * bq) - alpha * rq
    beta = rr / bb
    r_ar = rq - alpha * (bp - alpha * qp)
    b_ar = bq - alpha * bp
    curvature = r_ar + beta * (rq + b_ar) + beta * beta * bq
    gamma = rr / curvature
    b, q, p = vector[...], image[...], again[...]
    r = b - alpha * q
    d = r + beta * b
    ad = (q - alpha * p) + beta * q
    solution[...] = alpha * b + gamma * d
    residual[...] = r - gamma * ad


def shift(value, by):
    length = lax.axis_size(AXES)
    return lax.ppermute(value, AXES, [(i, i + by) for i in range(length) if 0 <= i + by < length])


def local(coords, noise, right_side, tiles, tile_count):
    blocks, width = right_side.shape
    reach = tiles.shape[1] - 1
    inner = sum(blocks - k for k in range(reach + 1))
    outer = reach * (reach + 1)

    first, last, packed = call(
        pack_kernel,
        (shape(reach, SUBLANES, width), shape(reach, SUBLANES, width), vmem(blocks, SUBLANES, width)),
        (tile_count, coords, right_side),
        [SMEM, VMEM, VMEM],
    )
    low = shift(last, 1)
    high = shift(first, -1)
    (packed,) = resident(packed)
    k_in, cols, accl, accs = call(
        functools.partial(inner_kernel, reach),
        (
            vmem(inner, width, width),
            vmem(4, blocks, width, LANES),
            vmem(blocks, width, LANES),
            vmem(blocks, SUBLANES, width),
        ),
        (tile_count, packed),
        [SMEM, VMEM],
        [vmem(blocks, SUBLANES, width)],
    )
    cols, accl, accs = resident(cols, accl, accs)
    k_out, image, first, last = call(
        functools.partial(outer_kernel, reach),
        (vmem(outer, width, width), shape(blocks, width), shape(reach, width), shape(reach, width)),
        (tile_count, low, high, packed, noise, cols, accl, accs),
        [SMEM] + [VMEM] * 7,
        [vmem(reach, SUBLANES, width), vmem(reach, SUBLANES, width), vmem(blocks, width, LANES)],
    )
    image_low = shift(last, 1)
    image_high = shift(first, -1)
    (k_in,) = resident(k_in)
    accl, accs = call(
        functools.partial(again_kernel, reach),
        (vmem(blocks, width, LANES), vmem(blocks, SUBLANES, width)),
        (tile_count, image, k_in),
        [SMEM, VMEM, VMEM],
        [vmem(blocks, SUBLANES, width), vmem(blocks, width, LANES)],
    )
    k_out, accl, accs = resident(k_out, accl, accs)
    devices = lax.axis_size(AXES)
    again, sums = call(
        functools.partial(close_kernel, reach),
        (shape(blocks, width), shape(devices, LANES)),
        (tile_count, image_low, image_high, low, right_side, noise, image, k_out, accl, accs),
        [SMEM] + [VMEM] * 9,
        [vmem(reach, SUBLANES, width), vmem(reach, SUBLANES, width), vmem(blocks, width, LANES)],
    )
    sums = lax.all_to_all(sums, AXES, 0, 0, tiled=True)
    return call(
        finish_kernel,
        (shape(blocks, width), shape(blocks, width)),
        (sums, right_side, image, again),
        [VMEM] * 4,
    )


def solution(mesh):
    in_specs = (
        P(("runs", "grp", "mem"), None, None),
        P(("runs", "grp", "mem"), None),
        P(("runs", "grp", "mem"), None),
        P(("runs", "grp", "mem"), None, None),
        P(("runs", "grp", "mem")),
    )
    out_specs = (P(("runs", "grp", "mem"), None), P(("runs", "grp", "mem"), None))
    return jax.shard_map(local, mesh=mesh, in_specs=in_specs, out_specs=out_specs, check_vma=False)
```

```python
import functools

import jax
import jax.numpy as jnp
from jax import lax
from jax.experimental import pallas as pl
from jax.experimental.pallas import tpu as pltpu
from jax.sharding import PartitionSpec as P

SCALE = 0.2 * 16.0
TINY = 1e-30
LANES = 128
SUBLANES = 8
BAND = 128
UNROLL = 16
AXES = ("grp", "mem")
MIB = 1 << 20
X, Y, T, V, N, COUNT = range(6)
NEAR = 4.0
PARTS = ((0, 0), (0, 1), (1, 0), (1, 1), (0, 2), (2, 0))
FEATURES = 32
FIRST_T = 2 * len(PARTS) + 6

VMEM = pl.BlockSpec(memory_space=pltpu.VMEM)
SMEM = pl.BlockSpec(memory_space=pltpu.SMEM)
HBM = pl.BlockSpec(memory_space=pltpu.HBM)


def resident(*arrays):
    return [pltpu.with_memory_space_constraint(a, pltpu.VMEM) for a in arrays]


def call(kernel, out_shape, operands, specs, scratch=(), limit=8, aliases=None):
    return pl.pallas_call(
        kernel,
        out_shape=out_shape,
        in_specs=specs,
        out_specs=jax.tree.map(lambda _: VMEM, out_shape),
        scratch_shapes=list(scratch),
        input_output_aliases=aliases or {},
        compiler_params=pltpu.CompilerParams(vmem_limit_bytes=limit * MIB),
    )(*operands)


def shape(*dims):
    return jax.ShapeDtypeStruct(dims, jnp.float32)


def vmem(*dims, dtype=jnp.float32):
    return pltpu.VMEM(dims, dtype)


def entries(u, ti, tj, mode):
    u = jnp.maximum(u, TINY)
    s = u * lax.rsqrt(u)
    a = jnp.maximum(1.0 - s, 0.0)
    if mode == "same":
        d = jnp.abs(ti - tj)
        b = 1.0 - d
        f = d + 0.25
    elif mode == "any":
        d = jnp.abs(ti - tj)
        b = jnp.maximum(1.0 - d, 0.0)
        f = d + 0.25
    else:
        b = jnp.maximum(ti - tj, 0.0)
        f = 1.25 - b
    p = a * b
    p = p * p
    return (p * p) * ((s + 0.25) * f)


def spread(row):
    return jnp.broadcast_to(row, (SUBLANES, row.shape[-1]))


def cut(ch):
    return slice(ch * LANES, (ch + 1) * LANES)


def split(a):
    high = a.astype(jnp.bfloat16).astype(jnp.float32)
    rest = a - high
    middle = rest.astype(jnp.bfloat16).astype(jnp.float32)
    return [high, middle, rest - middle]


def left_features(x, y):
    xs, ys, norm = split(x), split(y), split(x * x + y * y)
    one = jnp.ones_like(x)
    return [xs[i] for i, _ in PARTS] + [ys[i] for i, _ in PARTS] + norm + [one] * 3


def right_features(x, y):
    xs, ys, norm = split(x), split(y), split(x * x + y * y)
    one = jnp.ones_like(x)
    return [-2.0 * xs[j] for _, j in PARTS] + [-2.0 * ys[j] for _, j in PARTS] + [one] * 3 + norm


def put_right(rt, b, features, flat):
    flat[...] = jnp.zeros_like(flat)
    for q, z in enumerate(features):
        flat[q : q + 1, :] = z[b : b + 1, :]
    rt[b, 0:FEATURES, :] = flat[...].astype(jnp.bfloat16)


def columns(lt, firsts):
    dims = (LANES, LANES * len(firsts))
    row = lax.broadcasted_iota(jnp.int32, dims, 0)
    group = lax.broadcasted_iota(jnp.int32, dims, 1) // LANES
    pick = jnp.zeros(dims, jnp.float32)
    for n, first in enumerate(firsts):
        pick = jnp.where((group == n) & (row >= first) & (row < first + 3), 1.0, pick)
    return jnp.dot(lt, pick.astype(jnp.bfloat16), preferred_element_type=jnp.float32)


def near(x, y):
    return jnp.max(jnp.maximum(jnp.abs(x), jnp.abs(y))) <= NEAR


def new_tile(fill, code, following, mode, diag, side, k_ref, tcol, vcol, accl, accs, bufs):
    slot, r, c = code >> 8, (code >> 4) & 15, code & 15
    width = side.shape[-1]
    chunks = width // LANES
    bands = width // BAND
    tj, vj = [[spread(side[c, q : q + 1, cut(ch)]) for ch in range(chunks)] for q in (T, V)]
    zero = jnp.zeros((SUBLANES, LANES), jnp.float32)
    acc = [zero] * chunks
    for band in range(bands):
        first = band * BAND // LANES if diag else 0
        used = range(first, chunks)
        if band + 1 < bands:
            fill(bufs[(band + 1) % 2], r, c, band + 1, (band + 1) * BAND // LANES if diag else 0)
        else:
            fill(bufs[0], (following >> 4) & 15, following & 15, 0, 0)
        buf = bufs[band % 2]
        for g in range(BAND // SUBLANES):
            near_rows = slice(g * SUBLANES, (g + 1) * SUBLANES)
            at = slice(band * BAND + g * SUBLANES, band * BAND + (g + 1) * SUBLANES)
            ti = tcol[r, at, :]
            if mode == "next":
                ti = ti + 1.0
            if accs is not None:
                vi = vcol[r, at, :]
            total = None
            for ch in used:
                m = entries(buf[near_rows, cut(ch)], ti, tj[ch], mode)
                k_ref[slot, at, cut(ch)] = m
                w = m * vj[ch]
                total = w if total is None else total + w
                if accs is not None and not (diag and ch == first):
                    acc[ch] = acc[ch] + m * vi
            accl[r, at, :] += total
    if accs is not None:
        for ch in range(1 if diag else 0, chunks):
            accs[c, :, cut(ch)] += acc[ch]


def old_tile(code, side, k_ref, vcol, accl, accs, diag):
    slot, r, c = code >> 8, (code >> 4) & 15, code & 15
    width = side.shape[-1]
    chunks = width // LANES
    vj = [spread(side[c, 0:1, cut(ch)]) for ch in range(chunks)]
    zero = jnp.zeros((SUBLANES, LANES), jnp.float32)

    def rows_at(at, acc, used, single):
        acc = list(acc)
        if accs is not None:
            vi = vcol[r, at, :]
        total = None
        for q, ch in enumerate(used):
            m = k_ref[slot, at, cut(ch)]
            w = m * vj[ch]
            total = w if total is None else total + w
            if accs is not None and ch != single:
                acc[q] = acc[q] + m * vi
        accl[r, at, :] += total
        return tuple(acc)

    def band(lo, hi, used, single):
        def step(it, acc):
            for g in range(UNROLL):
                start = pl.multiple_of((it * UNROLL + g) * SUBLANES, SUBLANES)
                acc = rows_at(pl.ds(start, SUBLANES), acc, used, single)
            return acc

        deep = SUBLANES * UNROLL
        acc = lax.fori_loop(lo // deep, hi // deep, step, tuple(zero for _ in used))
        if accs is not None:
            for q, ch in enumerate(used):
                if ch != single:
                    accs[c, :, cut(ch)] += acc[q]

    if diag:
        for ri in range(chunks):
            band(ri * LANES, (ri + 1) * LANES, list(range(ri, chunks)), ri)
    else:
        band(0, width, list(range(chunks)), -1)


def list_inner(blocks, reach, count, todo):
    for r in range(blocks):
        todo[r] = (r << 8) | (r << 4) | r
    ends = [blocks]
    at = jnp.int32(blocks)
    base = 0
    for k in range(1, reach + 1):

        def step(r, at, k=k, base=base):
            todo[at] = ((base + r) << 8) | (r << 4) | (r + k)
            return at + (count[r] > k).astype(jnp.int32)

        at = lax.fori_loop(0, blocks - k, step, at)
        base += blocks - k
        if k == 1:
            ends.append(at)
            base = 0
    todo[at] = 0
    return ends + [at]


def list_outer(blocks, reach, count, low, todo):
    packed_count = jnp.zeros((1, LANES), jnp.float32)
    for at in range(reach):
        packed_count += low[at, COUNT : COUNT + 1, 0:LANES] * float(8**at)
    low_count = jnp.max(packed_count).astype(jnp.int32)
    at = jnp.int32(0)
    slot = 0
    for k in range(1, reach + 1):
        for j in range(k):
            c = reach - k + j
            todo[at] = (slot << 8) | (j << 4) | c
            at += (((low_count >> (3 * c)) & 7) > k).astype(jnp.int32)
            slot += 1
            r = blocks - k + j
            todo[at] = (slot << 8) | (r << 4) | (reach + j)
            at += (count[r] > k).astype(jnp.int32)
            slot += 1
    todo[at] = 0
    return at


def pack_kernel(count_in, coords_in, vector_in, noise_in, first, last, packed, count, coords, vector, noise, sems):
    blocks, _, width = packed.shape
    edge = first.shape[0]
    copies = [
        pltpu.make_async_copy(source, target, sems.at[n])
        for n, (source, target) in enumerate(
            [(count_in, count), (coords_in, coords), (vector_in, vector), (noise_in, noise)]
        )
    ]
    for copy in copies:
        copy.start()
    for copy in copies:
        copy.wait()
    for b in range(blocks):
        for q in (X, Y, T):
            packed[b, q : q + 1, :] = coords[q, b : b + 1, :]
        packed[b, V : V + 1, :] = vector[b : b + 1, :]
        packed[b, N : N + 1, :] = noise[b : b + 1, :]
        packed[b, COUNT:, :] = jnp.full((SUBLANES - COUNT, width), count[b].astype(jnp.float32))
    first[...] = packed[0:edge]
    last[...] = packed[blocks - edge :]


def rows_together(source, q):
    return jnp.concatenate([source[b, q : q + 1, :] for b in range(source.shape[0])], axis=0)


def centre(packed):
    head = packed[0, :, 0:LANES]
    mean = jnp.sum(head, axis=1, keepdims=True) * (1.0 / LANES)
    return mean[X : X + 1], mean[Y : Y + 1], jnp.floor(head[T : T + 1, 0:1])


def matmul_fill(lt, rt):
    def fill(buf, r, c, band, first):
        buf[:, first * LANES :] = jnp.dot(
            lt[r, band * BAND : (band + 1) * BAND, :],
            rt[c, :, first * LANES :],
            preferred_element_type=jnp.float32,
        )

    return fill


def difference_fill(packed, raw):
    def fill(buf, r, c, band, first):
        own = packed[r, :, band * BAND : (band + 1) * BAND].T
        dx = own[:, X : X + 1] - raw[c, X : X + 1, :]
        dy = own[:, Y : Y + 1] - raw[c, Y : Y + 1, :]
        buf[...] = dx * dx + dy * dy

    return fill


def inner_kernel(reach, count, packed, k_same, k_next, k_far, tcol, lt, accl, accs, vcol, rows, rt, flat, buf_a, buf_b, todo):
    blocks, _, width = packed.shape
    cx, cy, start = centre(packed)
    x, y = rows_together(packed, X) - cx, rows_together(packed, Y) - cy
    t, v = rows_together(packed, T) - start, rows_together(packed, V)
    left = left_features(x, y) + split(t) + split(v)
    right = right_features(x, y)
    rt[:, FEATURES:, :] = jnp.zeros((blocks, LANES - FEATURES, width), jnp.bfloat16)
    for b in range(blocks):
        rows[b, T : T + 1, :] = t[b : b + 1, :]
        rows[b, V : V + 1, :] = v[b : b + 1, :]
        flat[...] = jnp.zeros_like(flat)
        for q, z in enumerate(left):
            flat[q : q + 1, :] = z[b : b + 1, :]
        lt[b, :, 0:FEATURES] = flat[...].T.astype(jnp.bfloat16)
        lt[b, :, FEATURES:] = jnp.zeros((width, LANES - FEATURES), jnp.bfloat16)
        put_right(rt, b, right, flat)
    for b in range(blocks):
        both = columns(lt[b], (FIRST_T, FIRST_T + 3))
        tcol[b] = both[:, :LANES]
        vcol[b] = both[:, LANES:]
    accl[...] = jnp.zeros_like(accl)
    accs[...] = jnp.zeros_like(accs)
    ends = list_inner(blocks, reach, count, todo)
    bufs = (buf_a, buf_b)

    def run(fill):
        fill(buf_a, 0, 0, 0, 0)
        begin = 0
        for end, mode, k_ref in zip(ends, ("same", "any", "next"), (k_same, k_next, k_far)):

            def body(n, _, mode=mode, k_ref=k_ref):
                new_tile(fill, todo[n], todo[n + 1], mode, mode == "same", rows, k_ref, tcol, vcol, accl, accs, bufs)
                return 0

            lax.fori_loop(begin, end, body, 0)
            begin = end

    fast = near(x, y)
    pl.when(fast)(lambda: run(matmul_fill(lt, rt)))
    pl.when(jnp.logical_not(fast))(lambda: run(difference_fill(packed, packed)))


def outer_kernel(
    reach, count, low, high, packed, tcol, lt, accl_in, accs,
    kx, image, first, last, accl, raw, rows, rt, flat, buf_a, buf_b, todo,
):
    blocks, _, width = packed.shape
    halo = 2 * reach
    cx, cy, start = centre(packed)
    raw[0:reach] = low[...]
    raw[reach:] = high[...]
    x, y = rows_together(raw, X) - cx, rows_together(raw, Y) - cy
    t = rows_together(raw, T) - start
    right = right_features(x, y)
    rt[:, FEATURES:, :] = jnp.zeros((halo, LANES - FEATURES, width), jnp.bfloat16)
    for b in range(halo):
        rows[b, T : T + 1, :] = t[b : b + 1, :]
        rows[b, V : V + 1, :] = raw[b, V : V + 1, :]
        put_right(rt, b, right, flat)
    end = list_outer(blocks, reach, count, low, todo)
    bufs = (buf_a, buf_b)

    def run(fill):
        code = todo[0]
        fill(buf_a, (code >> 4) & 15, code & 15, 0, 0)

        def body(n, _):
            new_tile(fill, todo[n], todo[n + 1], "any", False, rows, kx, tcol, None, accl, None, bufs)
            return 0

        lax.fori_loop(0, end, body, 0)

    own = jnp.concatenate([rows_together(packed, X) - cx, rows_together(packed, Y) - cy], axis=0)
    fast = jnp.logical_and(near(x, y), near(own, own))
    pl.when(fast)(lambda: run(matmul_fill(lt, rt)))
    pl.when(jnp.logical_not(fast))(lambda: run(difference_fill(packed, raw)))
    summed = jnp.sum(accs[...], axis=1) + jnp.sum(accl[...], axis=-1)
    image[...] = rows_together(packed, N) * rows_together(packed, V) + SCALE * summed
    first[...] = image[0:reach, :]
    last[...] = image[blocks - reach :, :]


def again_kernel(reach, count, image, k_same, k_next, k_far, accl, accs, rows, vcol, flat, todo):
    blocks, width = image.shape
    flat[...] = jnp.zeros_like(flat)
    for n, part in enumerate(split(image[...])):
        for b in range(blocks):
            flat[3 * b + n : 3 * b + n + 1, :] = part[b : b + 1, :]
    lt = flat[...].T.astype(jnp.bfloat16)
    for b in range(blocks):
        rows[b, 0:1, :] = image[b : b + 1, :]
    for b in range(0, blocks, 2):
        both = columns(lt, (3 * b, 3 * b + 3))
        vcol[b] = both[:, :LANES]
        vcol[b + 1] = both[:, LANES:]
    accl[...] = jnp.zeros_like(accl)
    accs[...] = jnp.zeros_like(accs)
    ends = list_inner(blocks, reach, count, todo)
    begin = 0
    for end, k_ref in zip(ends, (k_same, k_next, k_far)):

        def body(n, _, k_ref=k_ref):
            old_tile(todo[n], rows, k_ref, vcol, accl, accs, k_ref is k_same)
            return 0

        lax.fori_loop(begin, end, body, 0)
        begin = end


def dots(pairs):
    lane = lax.broadcasted_iota(jnp.int32, (1, LANES), 1)
    out = jnp.zeros((1, LANES), jnp.float32)
    for n, (a, b) in enumerate(pairs):
        total = jnp.sum(jnp.sum(a * b, axis=1, keepdims=True), axis=0, keepdims=True)
        out = jnp.where(lane == n, total, out)
    return out


def close_kernel(reach, count, low_in, high_in, low, packed, image, kx, accl_in, accs, again, sums, accl, rows, todo):
    blocks = image.shape[0]
    for b in range(reach):
        rows[b, 0:1, :] = low_in[b : b + 1, :]
        rows[reach + b, 0:1, :] = high_in[b : b + 1, :]
    end = list_outer(blocks, reach, count, low, todo)

    def body(n, _):
        old_tile(todo[n], rows, kx, None, accl, None, False)
        return 0

    lax.fori_loop(0, end, body, 0)
    summed = jnp.sum(accs[...], axis=1) + jnp.sum(accl[...], axis=-1)
    q = image[...]
    p = rows_together(packed, N) * q + SCALE * summed
    again[...] = p
    b = rows_together(packed, V)
    sums[...] = jnp.broadcast_to(dots([(b, b), (b, q), (q, q), (b, p), (q, p)]), sums.shape)


def finish_kernel(sums, packed, image, again, solution, residual):
    total = jnp.sum(sums[...], axis=0, keepdims=True)
    bb, bq, qq, bp, qp = [total[:, n : n + 1] for n in range(5)]
    alpha = bb / bq
    rq = bq - alpha * qq
    rr = (bb - alpha * bq) - alpha * rq
    beta = rr / bb
    r_ar = rq - alpha * (bp - alpha * qp)
    b_ar = bq - alpha * bp
    curvature = r_ar + beta * (rq + b_ar) + beta * beta * bq
    gamma = rr / curvature
    b, q, p = rows_together(packed, V), image[...], again[...]
    r = b - alpha * q
    d = r + beta * b
    ad = (q - alpha * p) + beta * q
    solution[...] = alpha * b + gamma * d
    residual[...] = r - gamma * ad


def shift(value, by):
    length = lax.axis_size(AXES)
    return lax.ppermute(value, AXES, [(i, i + by) for i in range(length) if 0 <= i + by < length])


def local(coords, noise, right_side, tiles, tile_count):
    blocks, width = right_side.shape
    reach = tiles.shape[1] - 1
    inner = sum(blocks - k for k in range(reach + 1))
    outer = reach * (reach + 1)
    half = jnp.bfloat16
    bands = [vmem(BAND, width), vmem(BAND, width)]
    todo = pltpu.SMEM((inner + 2,), jnp.int32)

    first, last, packed = call(
        pack_kernel,
        (shape(reach, SUBLANES, width), shape(reach, SUBLANES, width), vmem(blocks, SUBLANES, width)),
        (tile_count, jnp.transpose(coords, (1, 0, 2)), right_side, noise),
        [HBM] * 4,
        [
            pltpu.SMEM((blocks,), jnp.int32),
            vmem(3, blocks, width),
            vmem(blocks, width),
            vmem(blocks, width),
            pltpu.SemaphoreType.DMA((4,)),
        ],
    )
    low = shift(last, 1)
    high = shift(first, -1)
    (packed,) = resident(packed)
    *k_in, tcol, lt, accl, accs = call(
        functools.partial(inner_kernel, reach),
        (
            vmem(blocks, width, width),
            vmem(blocks - 1, width, width),
            vmem(inner - 2 * blocks + 1, width, width),
            vmem(blocks, width, LANES),
            vmem(blocks, width, LANES, dtype=half),
            vmem(blocks, width, LANES),
            vmem(blocks, SUBLANES, width),
        ),
        (tile_count, packed),
        [SMEM, VMEM],
        [
            vmem(blocks, width, LANES),
            vmem(blocks, SUBLANES, width),
            vmem(blocks, LANES, width, dtype=half),
            vmem(FEATURES, width),
            *bands,
            todo,
        ],
    )
    *k_in, tcol, lt, accl, accs = resident(*k_in, tcol, lt, accl, accs)
    k_out, image, first, last, accl = call(
        functools.partial(outer_kernel, reach),
        (
            vmem(outer, width, width),
            vmem(blocks, width),
            shape(reach, width),
            shape(reach, width),
            vmem(blocks, width, LANES),
        ),
        (tile_count, low, high, packed, tcol, lt, accl, accs),
        [SMEM] + [VMEM] * 7,
        [
            vmem(2 * reach, SUBLANES, width),
            vmem(2 * reach, SUBLANES, width),
            vmem(2 * reach, LANES, width, dtype=half),
            vmem(FEATURES, width),
            *bands,
            todo,
        ],
        aliases={6: 4},
    )
    image_low = shift(last, 1)
    image_high = shift(first, -1)
    image, *k_in = resident(image, *k_in)
    accl, accs = call(
        functools.partial(again_kernel, reach),
        (vmem(blocks, width, LANES), vmem(blocks, SUBLANES, width)),
        (tile_count, image, *k_in),
        [SMEM] + [VMEM] * 4,
        [vmem(blocks, SUBLANES, width), vmem(blocks, width, LANES), vmem(LANES, width), todo],
    )
    k_out, accl, accs = resident(k_out, accl, accs)
    devices = lax.axis_size(AXES)
    again, sums, _ = call(
        functools.partial(close_kernel, reach),
        (vmem(blocks, width), shape(devices, LANES), vmem(blocks, width, LANES)),
        (tile_count, image_low, image_high, low, packed, image, k_out, accl, accs),
        [SMEM] + [VMEM] * 8,
        [vmem(2 * reach, SUBLANES, width), todo],
        aliases={7: 2},
    )
    sums = lax.all_to_all(sums, AXES, 0, 0, tiled=True)
    (again,) = resident(again)
    return call(
        finish_kernel,
        (shape(blocks, width), shape(blocks, width)),
        (sums, packed, image, again),
        [VMEM] * 4,
    )


def solution(mesh):
    in_specs = (
        P(("runs", "grp", "mem"), None, None),
        P(("runs", "grp", "mem"), None),
        P(("runs", "grp", "mem"), None),
        P(("runs", "grp", "mem"), None, None),
        P(("runs", "grp", "mem")),
    )
    out_specs = (P(("runs", "grp", "mem"), None), P(("runs", "grp", "mem"), None))
    return jax.shard_map(local, mesh=mesh, in_specs=in_specs, out_specs=out_specs, check_vma=False)
```

```python
import functools

import jax
import jax.numpy as jnp
from jax import lax
from jax.experimental import pallas as pl
from jax.experimental.pallas import tpu as pltpu
from jax.sharding import PartitionSpec as P

SCALE = 0.2 * 16.0
TINY = 1e-30
LANES = 128
SUBLANES = 8
BAND = 128
UNROLL = 16
AXES = ("grp", "mem")
MIB = 1 << 20
X, Y, T, V, N, COUNT = range(6)
NEAR = 4.0
PARTS = ((0, 0), (0, 1), (1, 0), (1, 1), (0, 2), (2, 0))
NORM = 2 * len(PARTS)
ONES, TIMES, VECTOR = NORM + 3, NORM + 6, NORM + 9
FEATURES = 32

VMEM = pl.BlockSpec(memory_space=pltpu.VMEM)
SMEM = pl.BlockSpec(memory_space=pltpu.SMEM)
HBM = pl.BlockSpec(memory_space=pltpu.HBM)


def resident(*arrays):
    return [pltpu.with_memory_space_constraint(a, pltpu.VMEM) for a in arrays]


def call(kernel, out_shape, operands, specs, scratch=(), limit=8, aliases=None):
    return pl.pallas_call(
        kernel,
        out_shape=out_shape,
        in_specs=specs,
        out_specs=jax.tree.map(lambda _: VMEM, out_shape),
        scratch_shapes=list(scratch),
        input_output_aliases=aliases or {},
        compiler_params=pltpu.CompilerParams(vmem_limit_bytes=limit * MIB),
    )(*operands)


def shape(*dims):
    return jax.ShapeDtypeStruct(dims, jnp.float32)


def vmem(*dims, dtype=jnp.float32):
    return pltpu.VMEM(dims, dtype)


def entries(u, ti, tj, mode):
    u = jnp.maximum(u, TINY)
    s = u * lax.rsqrt(u)
    a = jnp.maximum(1.0 - s, 0.0)
    if mode == "same":
        d = jnp.abs(ti - tj)
        b = 1.0 - d
        f = d + 0.25
    else:
        b = jnp.maximum(ti - tj, 0.0)
        f = 1.25 - b
    p = a * b
    p = p * p
    return (p * p) * ((s + 0.25) * f)


def spread(row):
    return jnp.broadcast_to(row, (SUBLANES, row.shape[-1]))


def cut(ch):
    return slice(ch * LANES, (ch + 1) * LANES)


def block_at(c):
    return pl.ds(pl.multiple_of(c * SUBLANES, SUBLANES), SUBLANES)


def each_block(q, stride=SUBLANES):
    return pl.ds(q, SUBLANES, stride=stride)


def gather(rows, q):
    return jnp.concatenate([rows[ch, each_block(q), :] for ch in range(rows.shape[0])], axis=1)


def scatter(rows, at, z, first=0):
    for ch in range(z.shape[-1] // LANES):
        rows[first + ch, at, :] = z[:, cut(ch)]


def split(a):
    high = a.astype(jnp.bfloat16).astype(jnp.float32)
    rest = a - high
    middle = rest.astype(jnp.bfloat16).astype(jnp.float32)
    return [high, middle, rest - middle]


def left_features(x, y, t, v):
    xs, ys, one = split(x), split(y), jnp.ones_like(x)
    products = [xs[i] for i, _ in PARTS] + [ys[i] for i, _ in PARTS]
    return products + split(x * x + y * y) + [one] * 3 + split(t) + split(v)


def put_right(rt, wide, x, y):
    wide[...] = jnp.zeros_like(wide)
    xs, ys, one = split(x), split(y), jnp.ones_like(x)
    products = [-2.0 * xs[j] for _, j in PARTS] + [-2.0 * ys[j] for _, j in PARTS]
    for q, z in enumerate(products + [one] * 3 + split(x * x + y * y)):
        scatter(wide, each_block(q, FEATURES), z)
    for b in range(rt.shape[0]):
        for n in range(wide.shape[0]):
            rt[b, :, cut(n)] = wide[n, b * FEATURES : (b + 1) * FEATURES, :].astype(jnp.bfloat16)


def columns(lt, first, pairs):
    dims = (lt.shape[-1], LANES * pairs)
    row = lax.broadcasted_iota(jnp.int32, dims, 0) - first
    group = lax.broadcasted_iota(jnp.int32, dims, 1) // LANES
    pick = jnp.where((row >= 3 * group) & (row < 3 * group + 3), 1.0, 0.0)
    return jnp.dot(lt, pick.astype(jnp.bfloat16), preferred_element_type=jnp.float32)


def near(x, y):
    return jnp.max(jnp.maximum(jnp.abs(x), jnp.abs(y))) <= NEAR


def new_tile(fill, code, following, mode, diag, side, sign_of, k_ref, tcol, vcol, accl, accs, bufs):
    slot, r, c = code >> 8, (code >> 4) & 15, code & 15
    chunks = side.shape[0]
    bands = chunks * LANES // BAND
    sign = 1.0 if mode == "same" else sign_of(c)
    vj = [spread(side[ch, block_at(c), :][V : V + 1]) for ch in range(chunks)]
    tj = [sign * spread(side[ch, block_at(c), :][T : T + 1]) for ch in range(chunks)]
    zero = jnp.zeros((SUBLANES, LANES), jnp.float32)
    acc = [zero] * chunks
    for band in range(bands):
        first = band * BAND // LANES if diag else 0
        if band + 1 < bands:
            fill(bufs[(band + 1) % 2], r, c, band + 1, (band + 1) * BAND // LANES if diag else 0)
        else:
            fill(bufs[0], (following >> 4) & 15, following & 15, 0, 0)
        buf = bufs[band % 2]
        for g in range(BAND // SUBLANES):
            near_rows = slice(g * SUBLANES, (g + 1) * SUBLANES)
            at = slice(band * BAND + g * SUBLANES, band * BAND + (g + 1) * SUBLANES)
            ti = tcol[r, at, :]
            if mode == "next":
                ti = sign * ti + 1.0
            if accs is not None:
                vi = vcol[r, at, :]
            total = None
            for ch in range(first, chunks):
                m = entries(buf[near_rows, cut(ch)], ti, tj[ch], mode)
                k_ref[slot, at, cut(ch)] = m
                w = m * vj[ch]
                total = w if total is None else total + w
                if accs is not None and not (diag and ch == first):
                    acc[ch] = acc[ch] + m * vi
            accl[r, at, :] += total
    if accs is not None:
        for ch in range(1 if diag else 0, chunks):
            accs[c, :, cut(ch)] += acc[ch]


def old_tile(code, row_of, k_ref, vcol, accl, accs, diag):
    slot, r, c = code >> 8, (code >> 4) & 15, code & 15
    width = k_ref.shape[-1]
    chunks = width // LANES
    vj = [spread(row_of(c, ch)) for ch in range(chunks)]
    zero = jnp.zeros((SUBLANES, LANES), jnp.float32)

    def rows_at(at, acc, used, single):
        acc = list(acc)
        if accs is not None:
            vi = vcol[r, at, :]
        total = None
        for q, ch in enumerate(used):
            m = k_ref[slot, at, cut(ch)]
            w = m * vj[ch]
            total = w if total is None else total + w
            if accs is not None and ch != single:
                acc[q] = acc[q] + m * vi
        accl[r, at, :] += total
        return tuple(acc)

    def band(lo, hi, used, single):
        def step(it, acc):
            for g in range(UNROLL):
                start = pl.multiple_of((it * UNROLL + g) * SUBLANES, SUBLANES)
                acc = rows_at(pl.ds(start, SUBLANES), acc, used, single)
            return acc

        deep = SUBLANES * UNROLL
        acc = lax.fori_loop(lo // deep, hi // deep, step, tuple(zero for _ in used))
        if accs is not None:
            for q, ch in enumerate(used):
                if ch != single:
                    accs[c, :, cut(ch)] += acc[q]

    if diag:
        for ri in range(chunks):
            band(ri * LANES, (ri + 1) * LANES, list(range(ri, chunks)), ri)
    else:
        band(0, width, list(range(chunks)), -1)


def inner_slots(blocks, reach):
    return sum(blocks - k for k in range(reach + 1))


def list_inner(blocks, reach, count, todo, same):
    for r in range(blocks):
        todo[r] = (r << 8) | (r << 4) | r
    at = jnp.int32(blocks)
    ends = [at]

    def put(at, r, k, base, keep):
        todo[at] = ((base + r) << 8) | (r << 4) | (r + k)
        return at + keep.astype(jnp.int32)

    def bit(r):
        return ((same >> r) & 1) == 1

    at = lax.fori_loop(0, blocks - 1, lambda r, at: put(at, r, 1, 0, (count[r] > 1) & bit(r)), at)
    ends.append(at)
    at = lax.fori_loop(0, blocks - 1, lambda r, at: put(at, r, 1, 0, (count[r] > 1) & ~bit(r)), at)
    ends.append(at)
    base = 0
    for k in range(2, reach + 1):
        at = lax.fori_loop(0, blocks - k, lambda r, at, k=k, base=base: put(at, r, k, base, count[r] > k), at)
        base += blocks - k
    todo[at] = 0
    return ends + [at]


def list_outer(blocks, reach, count, low_count, todo, same):
    tiles = []
    slot = 0
    for k in range(1, reach + 1):
        for j in range(k):
            c, r = reach - k + j, blocks - k + j
            tiles.append((k, 0, (slot << 8) | (j << 4) | c, ((low_count >> (3 * c)) & 7) > k))
            tiles.append((k, 1, ((slot + 1) << 8) | (r << 4) | (reach + j), count[r] > k))
            slot += 2
    at = jnp.int32(0)
    ends = []
    for wanted in (True, False):
        for k, which, code, keep in tiles:
            together = ((same >> which) & 1) == 1 if k == 1 else None
            if wanted and k > 1:
                continue
            if k == 1:
                keep = keep & (together if wanted else ~together)
            todo[at] = code
            at += keep.astype(jnp.int32)
        ends.append(at)
    todo[at] = 0
    return ends


def cell(rows, b):
    at = b * SUBLANES + T
    return jnp.floor(rows[0, at : at + 1, 0:1])


def as_scalar(value):
    return jnp.max(jnp.broadcast_to(value, (1, LANES))).astype(jnp.int32)


def flag(condition, weight):
    return jnp.where(condition, float(weight), 0.0)


def low_counts(low):
    total = jnp.zeros((1, 1), jnp.float32)
    for b in range(low.shape[1] // SUBLANES):
        at = b * SUBLANES + COUNT
        total += low[0, at : at + 1, 0:1] * float(8**b)
    return total


def pack_kernel(count_in, coords_in, vector_in, noise_in, first, last, packed, count, coords, vector, noise, sems):
    chunks = packed.shape[0]
    edge = first.shape[1]
    copies = [
        pltpu.make_async_copy(source, target, sems.at[n])
        for n, (source, target) in enumerate(
            [(count_in, count), (coords_in, coords), (vector_in, vector), (noise_in, noise)]
        )
    ]
    for copy in copies:
        copy.start()
    for copy in copies:
        copy.wait()
    for q in (X, Y, T):
        scatter(packed, each_block(q), coords[q])
    scatter(packed, each_block(V), vector[...])
    scatter(packed, each_block(N), noise[...])
    for b in range(vector.shape[0]):
        at = b * SUBLANES + COUNT
        value = jnp.full((chunks, SUBLANES - COUNT, LANES), count[b].astype(jnp.float32))
        packed[:, at : (b + 1) * SUBLANES, :] = value
    first[...] = packed[:, 0:edge, :]
    last[...] = packed[:, packed.shape[1] - edge :, :]


def centre(packed):
    head = packed[0, 0:SUBLANES, :]
    mean = jnp.sum(head, axis=1, keepdims=True) * (1.0 / LANES)
    return mean[X : X + 1], mean[Y : Y + 1], cell(packed, 0)


def matmul_fill(lt, rt):
    def fill(buf, r, c, band, first):
        own = lt[r, band * BAND : (band + 1) * BAND, :]
        at = slice(first * LANES, buf.shape[-1])
        buf[:, at] = jnp.dot(own, rt[c, :, at], preferred_element_type=jnp.float32)

    return fill


def difference_fill(packed, raw):
    def fill(buf, r, c, band, first):
        own = packed[band * BAND // LANES, block_at(r), :].T
        for ch in range(first, raw.shape[0]):
            other = raw[ch, block_at(c), :]
            dx, dy = [own[:, q : q + 1] - other[q : q + 1, :] for q in (X, Y)]
            buf[:, cut(ch)] = dx * dx + dy * dy

    return fill


def run_tiles(fill, todo, ends, modes, tile):
    code = todo[0]
    fill((code >> 4) & 15, code & 15)
    begin = 0
    for end, mode in zip(ends, modes):

        def body(n, _, mode=mode):
            tile(todo[n], todo[n + 1], mode)
            return 0

        lax.fori_loop(begin, end, body, 0)
        begin = end


def inner_kernel(
    reach, count, packed, k_same, k_next, k_far, tcol, lt, accl, accs, rows, vcol, flat, wide, rt, buf_a, buf_b, todo
):
    blocks = accs.shape[0]
    cx, cy, start = centre(packed)
    x, y = gather(packed, X) - cx, gather(packed, Y) - cy
    t, v = gather(packed, T) - start, gather(packed, V)
    flat[...] = jnp.zeros_like(flat)
    for q, z in enumerate(left_features(x, y, t, v)):
        scatter(flat, each_block(q, FEATURES), z)
    put_right(rt, wide, x, y)
    scatter(rows, each_block(T), t)
    scatter(rows, each_block(V), v)
    for b in range(blocks):
        for ch in range(flat.shape[0]):
            part = flat[ch, b * FEATURES : (b + 1) * FEATURES, :].T
            lt[b, cut(ch), :] = part.astype(jnp.bfloat16)
        both = columns(lt[b], TIMES, 2)
        tcol[b] = both[:, :LANES]
        vcol[b] = both[:, LANES:]
    accl[...] = jnp.zeros_like(accl)
    accs[...] = jnp.zeros_like(accs)
    same = jnp.zeros((1, 1), jnp.float32)
    for r in range(blocks - 1):
        same += flag(cell(packed, r) == cell(packed, r + 1), 1 << r)
    ends = list_inner(blocks, reach, count, todo, as_scalar(same))
    bufs = (buf_a, buf_b)
    kinds = (("same", k_same), ("same", k_next), ("next", k_next), ("next", k_far))

    def run(fill):
        def tile(code, following, kind):
            mode, k_ref = kind
            new_tile(
                fill, code, following, mode, k_ref is k_same,
                rows, lambda c: 1.0, k_ref, tcol, vcol, accl, accs, bufs,
            )

        run_tiles(lambda r, c: fill(buf_a, r, c, 0, 0), todo, ends, kinds, tile)

    fast = near(x, y)
    pl.when(fast)(lambda: run(matmul_fill(lt, rt)))
    pl.when(jnp.logical_not(fast))(lambda: run(difference_fill(packed, packed)))


def outer_kernel(
    reach, count, low, high, packed, tcol, lt, accl_in, accs,
    k_ref, image, first, last, accl, raw, rows, wide, rt, buf_a, buf_b, todo,
):
    blocks = accs.shape[0]
    edge = reach * SUBLANES
    cx, cy, start = centre(packed)
    raw[...] = jnp.zeros_like(raw)
    raw[:, 0:edge, :] = low[...]
    raw[:, edge : 2 * edge, :] = high[...]
    x, y = gather(raw, X) - cx, gather(raw, Y) - cy
    t = gather(raw, T) - start
    place = lax.broadcasted_iota(jnp.int32, (SUBLANES, 1), 0)
    put_right(rt, wide, x, y)
    scatter(rows, each_block(T), t)
    scatter(rows, each_block(V), gather(raw, V))
    scalars = low_counts(low)
    scalars += flag(cell(low, reach - 1) == cell(packed, 0), 1 << (3 * reach))
    scalars += flag(cell(packed, blocks - 1) == cell(high, 0), 1 << (3 * reach + 1))
    code = as_scalar(scalars)
    ends = list_outer(blocks, reach, count, code, todo, code >> (3 * reach))
    bufs = (buf_a, buf_b)

    def run(fill):
        def tile(code, following, mode):
            new_tile(
                fill, code, following, mode, False,
                rows, lambda c: jnp.where(c < reach, -1.0, 1.0), k_ref, tcol, None, accl, None, bufs,
            )

        run_tiles(lambda r, c: fill(buf_a, r, c, 0, 0), todo, ends, ("same", "next"), tile)

    halo = jnp.where(place < 2 * reach, 1.0, 0.0)
    own_x, own_y = gather(packed, X) - cx, gather(packed, Y) - cy
    reach_x = jnp.maximum(jnp.abs(x * halo), jnp.abs(own_x))
    reach_y = jnp.maximum(jnp.abs(y * halo), jnp.abs(own_y))
    fast = near(reach_x, reach_y)
    pl.when(fast)(lambda: run(matmul_fill(lt, rt)))
    pl.when(jnp.logical_not(fast))(lambda: run(difference_fill(packed, raw)))
    summed = jnp.sum(accs[...], axis=1) + jnp.sum(accl[...], axis=-1)
    image[...] = gather(packed, N) * gather(packed, V) + SCALE * summed
    first[...] = image[0:reach, :]
    last[...] = image[blocks - reach :, :]


def again_kernel(reach, count, image, k_same, k_next, k_far, accl, accs, rows, vcol, flat, todo):
    blocks, width = image.shape
    flat[...] = jnp.zeros_like(flat)
    for n, part in enumerate(split(image[...])):
        scatter(flat, pl.ds(n, blocks, stride=3), part)
    lt = jnp.concatenate([flat[ch].T for ch in range(flat.shape[0])], axis=0).astype(jnp.bfloat16)
    for b in range(blocks):
        rows[b, 0:1, :] = image[b : b + 1, :]
    for b in range(0, blocks, 2):
        both = columns(lt, 3 * b, 2)
        vcol[b] = both[:, :LANES]
        vcol[b + 1] = both[:, LANES:]
    accl[...] = jnp.zeros_like(accl)
    accs[...] = jnp.zeros_like(accs)
    ends = list_inner(blocks, reach, count, todo, jnp.int32(0))

    def row_of(c, ch):
        return rows[c, 0:1, cut(ch)]

    for begin, end, k_ref in ((0, ends[0], k_same), (ends[0], ends[2], k_next), (ends[2], ends[3], k_far)):

        def body(n, _, k_ref=k_ref):
            old_tile(todo[n], row_of, k_ref, vcol, accl, accs, k_ref is k_same)
            return 0

        lax.fori_loop(begin, end, body, 0)


def dots(pairs):
    lane = lax.broadcasted_iota(jnp.int32, (1, LANES), 1)
    out = jnp.zeros((1, LANES), jnp.float32)
    for n, (a, b) in enumerate(pairs):
        total = jnp.sum(jnp.sum(a * b, axis=1, keepdims=True), axis=0, keepdims=True)
        out = jnp.where(lane == n, total, out)
    return out


def close_kernel(reach, count, low_in, high_in, low, packed, image, k_ref, accl_in, accs, again, sums, accl, rows, todo):
    blocks = image.shape[0]
    for b in range(reach):
        rows[b, 0:1, :] = low_in[b : b + 1, :]
        rows[reach + b, 0:1, :] = high_in[b : b + 1, :]
    ends = list_outer(blocks, reach, count, as_scalar(low_counts(low)), todo, jnp.int32(0))

    def body(n, _):
        old_tile(todo[n], lambda c, ch: rows[c, 0:1, cut(ch)], k_ref, None, accl, None, False)
        return 0

    lax.fori_loop(0, ends[-1], body, 0)
    summed = jnp.sum(accs[...], axis=1) + jnp.sum(accl[...], axis=-1)
    q = image[...]
    p = gather(packed, N) * q + SCALE * summed
    again[...] = p
    b = gather(packed, V)
    sums[...] = jnp.broadcast_to(dots([(b, b), (b, q), (q, q), (b, p), (q, p)]), sums.shape)


def finish_kernel(sums, packed, image, again, solution, residual):
    total = jnp.sum(sums[...], axis=0, keepdims=True)
    bb, bq, qq, bp, qp = [total[:, n : n + 1] for n in range(5)]
    alpha = bb / bq
    rq = bq - alpha * qq
    rr = (bb - alpha * bq) - alpha * rq
    beta = rr / bb
    r_ar = rq - alpha * (bp - alpha * qp)
    b_ar = bq - alpha * bp
    curvature = r_ar + beta * (rq + b_ar) + beta * beta * bq
    gamma = rr / curvature
    b, q, p = gather(packed, V), image[...], again[...]
    r = b - alpha * q
    d = r + beta * b
    ad = (q - alpha * p) + beta * q
    solution[...] = alpha * b + gamma * d
    residual[...] = r - gamma * ad


def shift(value, by):
    length = lax.axis_size(AXES)
    return lax.ppermute(value, AXES, [(i, i + by) for i in range(length) if 0 <= i + by < length])


def local(coords, noise, right_side, tiles, tile_count):
    blocks, width = right_side.shape
    reach = tiles.shape[1] - 1
    chunks = width // LANES
    edge = (chunks, reach * SUBLANES, LANES)
    half = jnp.bfloat16
    inner = inner_slots(blocks, reach) - blocks
    bands = [vmem(BAND, width), vmem(BAND, width)]
    factors = [vmem(chunks, SUBLANES * FEATURES, LANES), vmem(SUBLANES, FEATURES, width, dtype=half)]
    rows = vmem(chunks, SUBLANES * SUBLANES, LANES)
    todo = pltpu.SMEM((inner + blocks + 2,), jnp.int32)

    operands = (tile_count, jnp.transpose(coords, (1, 0, 2)), right_side, noise)
    first, last, packed = call(
        pack_kernel,
        (shape(*edge), shape(*edge), vmem(chunks, blocks * SUBLANES, LANES)),
        [pltpu.with_memory_space_constraint(a, pltpu.HBM) for a in operands],
        [HBM] * 4,
        [
            pltpu.SMEM((blocks,), jnp.int32),
            vmem(3, blocks, width),
            vmem(blocks, width),
            vmem(blocks, width),
            pltpu.SemaphoreType.DMA((4,)),
        ],
    )
    low = shift(last, 1)
    high = shift(first, -1)
    (packed,) = resident(packed)
    *k_in, tcol, lt, accl, accs = call(
        functools.partial(inner_kernel, reach),
        (
            vmem(blocks, width, width),
            vmem(blocks - 1, width, width),
            vmem(inner - blocks + 1, width, width),
            vmem(blocks, width, LANES),
            vmem(blocks, width, FEATURES, dtype=half),
            vmem(blocks, width, LANES),
            vmem(blocks, SUBLANES, width),
        ),
        (tile_count, packed),
        [SMEM, VMEM],
        [rows, vmem(blocks, width, LANES), vmem(chunks, blocks * FEATURES, LANES), *factors, *bands, todo],
    )
    *k_in, tcol, lt, accl, accs = resident(*k_in, tcol, lt, accl, accs)
    k_out, image, first, last, accl = call(
        functools.partial(outer_kernel, reach),
        (
            vmem(reach * (reach + 1), width, width),
            vmem(blocks, width),
            shape(reach, width),
            shape(reach, width),
            vmem(blocks, width, LANES),
        ),
        (tile_count, low, high, packed, tcol, lt, accl, accs),
        [SMEM] + [VMEM] * 7,
        [rows, rows, *factors, *bands, todo],
        aliases={6: 4},
    )
    image_low = shift(last, 1)
    image_high = shift(first, -1)
    image, *k_in = resident(image, *k_in)
    accl, accs = call(
        functools.partial(again_kernel, reach),
        (vmem(blocks, width, LANES), vmem(blocks, SUBLANES, width)),
        (tile_count, image, *k_in),
        [SMEM] + [VMEM] * 4,
        [vmem(blocks, SUBLANES, width), vmem(blocks, width, LANES), vmem(chunks, LANES, LANES), todo],
    )
    k_out, accl, accs = resident(k_out, accl, accs)
    devices = lax.axis_size(AXES)
    again, sums, _ = call(
        functools.partial(close_kernel, reach),
        (vmem(blocks, width), shape(devices, LANES), vmem(blocks, width, LANES)),
        (tile_count, image_low, image_high, low, packed, image, k_out, accl, accs),
        [SMEM] + [VMEM] * 8,
        [vmem(2 * reach, SUBLANES, width), todo],
        aliases={7: 2},
    )
    sums = lax.all_to_all(sums, AXES, 0, 0, tiled=True)
    (again,) = resident(again)
    return call(
        finish_kernel,
        (shape(blocks, width), shape(blocks, width)),
        (sums, packed, image, again),
        [VMEM] * 4,
    )


def solution(mesh):
    in_specs = (
        P(("runs", "grp", "mem"), None, None),
        P(("runs", "grp", "mem"), None),
        P(("runs", "grp", "mem"), None),
        P(("runs", "grp", "mem"), None, None),
        P(("runs", "grp", "mem")),
    )
    out_specs = (P(("runs", "grp", "mem"), None), P(("runs", "grp", "mem"), None))
    return jax.shard_map(local, mesh=mesh, in_specs=in_specs, out_specs=out_specs, check_vma=False)
```

```python
import functools

import jax
import jax.numpy as jnp
from jax import lax
from jax.experimental import pallas as pl
from jax.experimental.pallas import tpu as pltpu
from jax.sharding import PartitionSpec as P

SCALE = 0.2 * 16.0
TINY = 1e-30
LANES = 128
SUBLANES = 8
BAND = 128
UNROLL = 16
AXES = ("grp", "mem")
MIB = 1 << 20
X, Y, T, V, N, COUNT, ODD = range(7)
NEAR = 4.0
PARTS = ((0, 0), (0, 1), (1, 0), (1, 1), (0, 2), (2, 0))
NORM = 2 * len(PARTS)
ONES, TIMES, VECTOR = NORM + 3, NORM + 6, NORM + 9
FEATURES = 32

VMEM = pl.BlockSpec(memory_space=pltpu.VMEM)
SMEM = pl.BlockSpec(memory_space=pltpu.SMEM)
HBM = pl.BlockSpec(memory_space=pltpu.HBM)


def resident(*arrays):
    return [pltpu.with_memory_space_constraint(a, pltpu.VMEM) for a in arrays]


def call(kernel, out_shape, operands, specs, scratch=(), limit=8, aliases=None):
    return pl.pallas_call(
        kernel,
        out_shape=out_shape,
        in_specs=specs,
        out_specs=jax.tree.map(lambda _: VMEM, out_shape),
        scratch_shapes=list(scratch),
        input_output_aliases=aliases or {},
        compiler_params=pltpu.CompilerParams(vmem_limit_bytes=limit * MIB),
    )(*operands)


def shape(*dims):
    return jax.ShapeDtypeStruct(dims, jnp.float32)


def vmem(*dims, dtype=jnp.float32):
    return pltpu.VMEM(dims, dtype)


def entries(u, ti, tj, mode):
    u = jnp.maximum(u, TINY)
    s = u * lax.rsqrt(u)
    a = jnp.maximum(1.0 - s, 0.0)
    if mode == "same":
        d = jnp.abs(ti - tj)
        b = 1.0 - d
        f = d + 0.25
    else:
        b = jnp.maximum(ti - tj, 0.0)
        f = 1.25 - b
    p = a * b
    p = p * p
    return (p * p) * ((s + 0.25) * f)


def spread(row):
    return jnp.broadcast_to(row, (SUBLANES, row.shape[-1]))


def cut(ch):
    return slice(ch * LANES, (ch + 1) * LANES)


def block_at(c):
    return pl.ds(pl.multiple_of(c * SUBLANES, SUBLANES), SUBLANES)


def each_block(q, stride=SUBLANES):
    return pl.ds(q, SUBLANES, stride=stride)


def gather(rows, q):
    return jnp.concatenate([rows[ch, each_block(q), :] for ch in range(rows.shape[0])], axis=1)


def scatter(rows, at, z, first=0):
    for ch in range(z.shape[-1] // LANES):
        rows[first + ch, at, :] = z[:, cut(ch)]


def split(a):
    high = a.astype(jnp.bfloat16).astype(jnp.float32)
    rest = a - high
    middle = rest.astype(jnp.bfloat16).astype(jnp.float32)
    return [high, middle, rest - middle]


def left_features(x, y, t, v):
    xs, ys, one = split(x), split(y), jnp.ones_like(x)
    products = [xs[i] for i, _ in PARTS] + [ys[i] for i, _ in PARTS]
    return products + split(x * x + y * y) + [one] * 3 + split(t) + split(v)


def put_right(rt, wide, x, y):
    wide[...] = jnp.zeros_like(wide)
    xs, ys, one = split(x), split(y), jnp.ones_like(x)
    products = [-2.0 * xs[j] for _, j in PARTS] + [-2.0 * ys[j] for _, j in PARTS]
    for q, z in enumerate(products + [one] * 3 + split(x * x + y * y)):
        scatter(wide, each_block(q, FEATURES), z)
    for b in range(rt.shape[0]):
        for n in range(wide.shape[0]):
            rt[b, :, cut(n)] = wide[n, b * FEATURES : (b + 1) * FEATURES, :].astype(jnp.bfloat16)


def columns(lt, first, pairs):
    dims = (lt.shape[-1], LANES * pairs)
    row = lax.broadcasted_iota(jnp.int32, dims, 0) - first
    group = lax.broadcasted_iota(jnp.int32, dims, 1) // LANES
    pick = jnp.where((row >= 3 * group) & (row < 3 * group + 3), 1.0, 0.0)
    return jnp.dot(lt, pick.astype(jnp.bfloat16), preferred_element_type=jnp.float32)


def near(x, y):
    return jnp.max(jnp.maximum(jnp.abs(x), jnp.abs(y))) <= NEAR


def new_tile(fill, code, following, mode, diag, side, sign_of, k_ref, tcol, vcol, accl, accs, bufs):
    slot, r, c = code >> 8, (code >> 4) & 15, code & 15
    chunks = side.shape[0]
    bands = chunks * LANES // BAND
    sign = 1.0 if mode == "same" else sign_of(c)
    vj = [spread(side[ch, block_at(c), :][V : V + 1]) for ch in range(chunks)]
    tj = [sign * spread(side[ch, block_at(c), :][T : T + 1]) for ch in range(chunks)]
    zero = jnp.zeros((SUBLANES, LANES), jnp.float32)
    acc = [zero] * chunks
    for band in range(bands):
        first = band * BAND // LANES if diag else 0
        if band + 1 < bands:
            fill(bufs[(band + 1) % 2], r, c, band + 1, (band + 1) * BAND // LANES if diag else 0)
        else:
            fill(bufs[0], (following >> 4) & 15, following & 15, 0, 0)
        buf = bufs[band % 2]
        for g in range(BAND // SUBLANES):
            near_rows = slice(g * SUBLANES, (g + 1) * SUBLANES)
            at = slice(band * BAND + g * SUBLANES, band * BAND + (g + 1) * SUBLANES)
            ti = tcol[r, at, :]
            if mode == "next":
                ti = sign * ti + 1.0
            if accs is not None:
                vi = vcol[r, at, :]
            total = None
            for ch in range(first, chunks):
                m = entries(buf[near_rows, cut(ch)], ti, tj[ch], mode)
                k_ref[slot, at, cut(ch)] = m
                w = m * vj[ch]
                total = w if total is None else total + w
                if accs is not None and not (diag and ch == first):
                    acc[ch] = acc[ch] + m * vi
            accl[r, at, :] = total if diag else accl[r, at, :] + total
    if accs is not None:
        for ch in range(1 if diag else 0, chunks):
            accs[c, :, cut(ch)] += acc[ch]


def old_tile(code, row_of, k_ref, vcol, accl, accs, diag):
    slot, r, c = code >> 8, (code >> 4) & 15, code & 15
    width = k_ref.shape[-1]
    chunks = width // LANES
    vj = [spread(row_of(c, ch)) for ch in range(chunks)]
    zero = jnp.zeros((SUBLANES, LANES), jnp.float32)

    def rows_at(at, acc, used, single):
        acc = list(acc)
        if accs is not None:
            vi = vcol[r, at, :]
        total = None
        for q, ch in enumerate(used):
            m = k_ref[slot, at, cut(ch)]
            w = m * vj[ch]
            total = w if total is None else total + w
            if accs is not None and ch != single:
                acc[q] = acc[q] + m * vi
        accl[r, at, :] = total if diag else accl[r, at, :] + total
        return tuple(acc)

    def band(lo, hi, used, single):
        def step(it, acc):
            for g in range(UNROLL):
                start = pl.multiple_of((it * UNROLL + g) * SUBLANES, SUBLANES)
                acc = rows_at(pl.ds(start, SUBLANES), acc, used, single)
            return acc

        deep = SUBLANES * UNROLL
        acc = lax.fori_loop(lo // deep, hi // deep, step, tuple(zero for _ in used))
        if accs is not None:
            for q, ch in enumerate(used):
                if ch != single:
                    accs[c, :, cut(ch)] += acc[q]

    if diag:
        for ri in range(chunks):
            band(ri * LANES, (ri + 1) * LANES, list(range(ri, chunks)), ri)
    else:
        band(0, width, list(range(chunks)), -1)


def inner_slots(blocks, reach):
    return sum(blocks - k for k in range(reach + 1))


def list_inner(blocks, reach, count, todo, same):
    for r in range(blocks):
        todo[r] = (r << 8) | (r << 4) | r
    at = jnp.int32(blocks)
    ends = [at]

    def put(at, r, k, base, keep):
        todo[at] = ((base + r) << 8) | (r << 4) | (r + k)
        return at + keep.astype(jnp.int32)

    def bit(r):
        return ((same >> r) & 1) == 1

    at = lax.fori_loop(0, blocks - 1, lambda r, at: put(at, r, 1, 0, (count[r] > 1) & bit(r)), at)
    ends.append(at)
    at = lax.fori_loop(0, blocks - 1, lambda r, at: put(at, r, 1, 0, (count[r] > 1) & ~bit(r)), at)
    ends.append(at)
    base = 0
    for k in range(2, reach + 1):
        at = lax.fori_loop(0, blocks - k, lambda r, at, k=k, base=base: put(at, r, k, base, count[r] > k), at)
        base += blocks - k
    todo[at] = 0
    return ends + [at]


def list_outer(blocks, reach, count, low_count, todo, same):
    tiles = []
    slot = 0
    for k in range(1, reach + 1):
        for j in range(k):
            c, r = reach - k + j, blocks - k + j
            tiles.append((k, 0, (slot << 8) | (j << 4) | c, ((low_count >> (3 * c)) & 7) > k))
            tiles.append((k, 1, ((slot + 1) << 8) | (r << 4) | (reach + j), count[r] > k))
            slot += 2
    at = jnp.int32(0)
    ends = []
    for wanted in (True, False):
        for k, which, code, keep in tiles:
            together = ((same >> which) & 1) == 1 if k == 1 else None
            if wanted and k > 1:
                continue
            if k == 1:
                keep = keep & (together if wanted else ~together)
            todo[at] = code
            at += keep.astype(jnp.int32)
        ends.append(at)
    todo[at] = 0
    return ends


def cell(rows, b):
    at = b * SUBLANES + T
    return jnp.floor(rows[0, at : at + 1, 0:1])


def as_scalar(value):
    return jnp.max(jnp.broadcast_to(value, (1, LANES))).astype(jnp.int32)


def flag(condition, weight):
    return jnp.where(condition, float(weight), 0.0)


def low_counts(low):
    total = jnp.zeros((1, 1), jnp.float32)
    for b in range(low.shape[1] // SUBLANES):
        at = b * SUBLANES + COUNT
        total += low[0, at : at + 1, 0:1] * float(8**b)
    return total


def pack_kernel(count_in, coords_in, vector_in, noise_in, even_out, odd_out, packed, count, coords, vector, noise, sems):
    chunks = packed.shape[0]
    edge = even_out.shape[1]
    odd = lax.rem(position(), 2).astype(jnp.float32)
    copies = [
        pltpu.make_async_copy(source, target, sems.at[n])
        for n, (source, target) in enumerate(
            [(count_in, count), (coords_in, coords), (vector_in, vector), (noise_in, noise)]
        )
    ]
    for copy in copies:
        copy.start()
    for copy in copies:
        copy.wait()
    for q in (X, Y, T):
        scatter(packed, each_block(q), coords[q])
    scatter(packed, each_block(V), vector[...])
    scatter(packed, each_block(N), noise[...])
    for b in range(vector.shape[0]):
        at = b * SUBLANES + COUNT
        packed[:, at : at + 1, :] = jnp.full((chunks, 1, LANES), count[b].astype(jnp.float32))
        packed[:, at + 1 : (b + 1) * SUBLANES, :] = jnp.full((chunks, SUBLANES - ODD, LANES), odd)
    first, last = packed[:, 0:edge, :], packed[:, packed.shape[1] - edge :, :]
    even_out[...], odd_out[...] = by_parity(packed, last, first)


def centre(packed):
    head = packed[0, 0:SUBLANES, :]
    mean = jnp.sum(head, axis=1, keepdims=True) * (1.0 / LANES)
    return mean[X : X + 1], mean[Y : Y + 1], cell(packed, 0)


def matmul_fill(lt, rt):
    def fill(buf, r, c, band, first):
        own = lt[r, band * BAND : (band + 1) * BAND, :]
        at = slice(first * LANES, buf.shape[-1])
        buf[:, at] = jnp.dot(own, rt[c, :, at], preferred_element_type=jnp.float32)

    return fill


def difference_fill(packed, raw):
    def fill(buf, r, c, band, first):
        own = packed[band * BAND // LANES, block_at(r), :].T
        for ch in range(first, raw.shape[0]):
            other = raw[ch, block_at(c), :]
            dx, dy = [own[:, q : q + 1] - other[q : q + 1, :] for q in (X, Y)]
            buf[:, cut(ch)] = dx * dx + dy * dy

    return fill


def run_tiles(fill, todo, ends, modes, tile):
    code = todo[0]
    fill((code >> 4) & 15, code & 15)
    begin = 0
    for end, mode in zip(ends, modes):

        def body(n, _, mode=mode):
            tile(todo[n], todo[n + 1], mode)
            return 0

        lax.fori_loop(begin, end, body, 0)
        begin = end


def inner_kernel(
    reach, count, packed, k_same, k_next, k_far, tcol, lt, accl, accs, rows, vcol, flat, wide, rt, buf_a, buf_b, todo
):
    blocks = accs.shape[0]
    cx, cy, start = centre(packed)
    x, y = gather(packed, X) - cx, gather(packed, Y) - cy
    t, v = gather(packed, T) - start, gather(packed, V)
    flat[...] = jnp.zeros_like(flat)
    for q, z in enumerate(left_features(x, y, t, v)):
        scatter(flat, each_block(q, FEATURES), z)
    put_right(rt, wide, x, y)
    scatter(rows, each_block(T), t)
    scatter(rows, each_block(V), v)
    for b in range(blocks):
        for ch in range(flat.shape[0]):
            part = flat[ch, b * FEATURES : (b + 1) * FEATURES, :].T
            lt[b, cut(ch), :] = part.astype(jnp.bfloat16)
        both = columns(lt[b], TIMES, 2)
        tcol[b] = both[:, :LANES]
        vcol[b] = both[:, LANES:]
    accs[...] = jnp.zeros_like(accs)
    same = jnp.zeros((1, 1), jnp.float32)
    for r in range(blocks - 1):
        same += flag(cell(packed, r) == cell(packed, r + 1), 1 << r)
    ends = list_inner(blocks, reach, count, todo, as_scalar(same))
    bufs = (buf_a, buf_b)
    kinds = (("same", k_same), ("same", k_next), ("next", k_next), ("next", k_far))

    def run(fill):
        def tile(code, following, kind):
            mode, k_ref = kind
            new_tile(
                fill, code, following, mode, k_ref is k_same,
                rows, lambda c: 1.0, k_ref, tcol, vcol, accl, accs, bufs,
            )

        run_tiles(lambda r, c: fill(buf_a, r, c, 0, 0), todo, ends, kinds, tile)

    fast = near(x, y)
    pl.when(fast)(lambda: run(matmul_fill(lt, rt)))
    pl.when(jnp.logical_not(fast))(lambda: run(difference_fill(packed, packed)))


def outer_kernel(
    reach, count, with_even, with_odd, packed, tcol, lt, accl_in, accs,
    k_ref, image, even_out, odd_out, accl, listed, raw, rows, wide, rt, buf_a, buf_b, todo,
):
    blocks = accs.shape[0]
    edge = reach * SUBLANES
    cx, cy, start = centre(packed)
    raw[...] = jnp.zeros_like(raw)
    high, low = by_parity(packed, with_even[...], with_odd[...])
    raw[:, 0:edge, :] = low
    raw[:, edge : 2 * edge, :] = high
    x, y = gather(raw, X) - cx, gather(raw, Y) - cy
    t = gather(raw, T) - start
    place = lax.broadcasted_iota(jnp.int32, (SUBLANES, 1), 0)
    put_right(rt, wide, x, y)
    scatter(rows, each_block(T), t)
    scatter(rows, each_block(V), gather(raw, V))
    scalars = low_counts(low)
    listed[...] = jnp.broadcast_to(scalars, listed.shape)
    scalars += flag(cell(low, reach - 1) == cell(packed, 0), 1 << (3 * reach))
    scalars += flag(cell(packed, blocks - 1) == cell(high, 0), 1 << (3 * reach + 1))
    code = as_scalar(scalars)
    ends = list_outer(blocks, reach, count, code, todo, code >> (3 * reach))
    bufs = (buf_a, buf_b)

    def run(fill):
        def tile(code, following, mode):
            new_tile(
                fill, code, following, mode, False,
                rows, lambda c: jnp.where(c < reach, -1.0, 1.0), k_ref, tcol, None, accl, None, bufs,
            )

        run_tiles(lambda r, c: fill(buf_a, r, c, 0, 0), todo, ends, ("same", "next"), tile)

    halo = jnp.where(place < 2 * reach, 1.0, 0.0)
    own_x, own_y = gather(packed, X) - cx, gather(packed, Y) - cy
    reach_x = jnp.maximum(jnp.abs(x * halo), jnp.abs(own_x))
    reach_y = jnp.maximum(jnp.abs(y * halo), jnp.abs(own_y))
    fast = near(reach_x, reach_y)
    pl.when(fast)(lambda: run(matmul_fill(lt, rt)))
    pl.when(jnp.logical_not(fast))(lambda: run(difference_fill(packed, raw)))
    summed = jnp.sum(accs[...], axis=1) + jnp.sum(accl[...], axis=-1)
    image[...] = gather(packed, N) * gather(packed, V) + SCALE * summed
    even_out[...], odd_out[...] = by_parity(packed, image[blocks - reach :, :], image[0:reach, :])


def again_kernel(reach, count, image, k_same, k_next, k_far, accl, accs, rows, vcol, flat, todo):
    blocks, width = image.shape
    flat[...] = jnp.zeros_like(flat)
    for n, part in enumerate(split(image[...])):
        scatter(flat, pl.ds(n, blocks, stride=3), part)
    lt = jnp.concatenate([flat[ch].T for ch in range(flat.shape[0])], axis=0).astype(jnp.bfloat16)
    for b in range(blocks):
        rows[b, 0:1, :] = image[b : b + 1, :]
    for b in range(0, blocks, 2):
        both = columns(lt, 3 * b, 2)
        vcol[b] = both[:, :LANES]
        vcol[b + 1] = both[:, LANES:]
    accs[...] = jnp.zeros_like(accs)
    ends = list_inner(blocks, reach, count, todo, jnp.int32(0))

    def row_of(c, ch):
        return rows[c, 0:1, cut(ch)]

    for begin, end, k_ref in ((0, ends[0], k_same), (ends[0], ends[2], k_next), (ends[2], ends[3], k_far)):

        def body(n, _, k_ref=k_ref):
            old_tile(todo[n], row_of, k_ref, vcol, accl, accs, k_ref is k_same)
            return 0

        lax.fori_loop(begin, end, body, 0)


def dots(pairs):
    lane = lax.broadcasted_iota(jnp.int32, (1, LANES), 1)
    out = jnp.zeros((1, LANES), jnp.float32)
    for n, (a, b) in enumerate(pairs):
        total = jnp.sum(jnp.sum(a * b, axis=1, keepdims=True), axis=0, keepdims=True)
        out = jnp.where(lane == n, total, out)
    return out


def close_kernel(
    reach, count, with_even, with_odd, listed, packed, image, k_ref, accl_in, accs, again, sums, accl, rows, todo
):
    blocks = image.shape[0]
    high, low = by_parity(packed, with_even[...], with_odd[...])
    for b in range(reach):
        rows[b, 0:1, :] = low[b : b + 1, :]
        rows[reach + b, 0:1, :] = high[b : b + 1, :]
    ends = list_outer(blocks, reach, count, as_scalar(listed[0:1, :]), todo, jnp.int32(0))

    def body(n, _):
        old_tile(todo[n], lambda c, ch: rows[c, 0:1, cut(ch)], k_ref, None, accl, None, False)
        return 0

    lax.fori_loop(0, ends[-1], body, 0)
    summed = jnp.sum(accs[...], axis=1) + jnp.sum(accl[...], axis=-1)
    q = image[...]
    p = gather(packed, N) * q + SCALE * summed
    again[...] = p
    b = gather(packed, V)
    sums[...] = jnp.broadcast_to(dots([(b, b), (b, q), (q, q), (b, p), (q, p)]), sums.shape)


def finish_kernel(sums, packed, image, again, solution, residual):
    total = jnp.sum(sums[...], axis=0, keepdims=True)
    bb, bq, qq, bp, qp = [total[:, n : n + 1] for n in range(5)]
    alpha = bb / bq
    rq = bq - alpha * qq
    rr = (bb - alpha * bq) - alpha * rq
    beta = rr / bb
    r_ar = rq - alpha * (bp - alpha * qp)
    b_ar = bq - alpha * bp
    curvature = r_ar + beta * (rq + b_ar) + beta * beta * bq
    gamma = rr / curvature
    b, q, p = gather(packed, V), image[...], again[...]
    r = b - alpha * q
    d = r + beta * b
    ad = (q - alpha * p) + beta * q
    solution[...] = alpha * b + gamma * d
    residual[...] = r - gamma * ad


def position():
    place = 0
    for axis in AXES:
        place = place * lax.axis_size(axis) + lax.axis_index(axis)
    return place


def by_parity(packed, low, high):
    odd = packed[0, ODD : ODD + 1, 0:1] > 0.5
    return jnp.where(odd, high, low), jnp.where(odd, low, high)


def swap(value, start):
    pairs = [(i, i + 1) for i in range(start, lax.axis_size(AXES) - 1, 2)]
    return lax.ppermute(value, AXES, pairs + [(b, a) for a, b in pairs])


def local(coords, noise, right_side, tiles, tile_count):
    blocks, width = right_side.shape
    reach = tiles.shape[1] - 1
    chunks = width // LANES
    edge = (chunks, reach * SUBLANES, LANES)
    half = jnp.bfloat16
    inner = inner_slots(blocks, reach) - blocks
    bands = [vmem(BAND, width), vmem(BAND, width)]
    factors = [vmem(chunks, SUBLANES * FEATURES, LANES), vmem(SUBLANES, FEATURES, width, dtype=half)]
    rows = vmem(chunks, SUBLANES * SUBLANES, LANES)
    todo = pltpu.SMEM((inner + blocks + 2,), jnp.int32)

    operands = (tile_count, jnp.transpose(coords, (1, 0, 2)), right_side, noise)
    even_out, odd_out, packed = call(
        pack_kernel,
        (shape(*edge), shape(*edge), vmem(chunks, blocks * SUBLANES, LANES)),
        [pltpu.with_memory_space_constraint(a, pltpu.HBM) for a in operands],
        [HBM] * 4,
        [
            pltpu.SMEM((blocks,), jnp.int32),
            vmem(3, blocks, width),
            vmem(blocks, width),
            vmem(blocks, width),
            pltpu.SemaphoreType.DMA((4,)),
        ],
    )
    with_even, with_odd = swap(even_out, 0), swap(odd_out, 1)
    (packed,) = resident(packed)
    *k_in, tcol, lt, accl, accs = call(
        functools.partial(inner_kernel, reach),
        (
            vmem(blocks, width, width),
            vmem(blocks - 1, width, width),
            vmem(inner - blocks + 1, width, width),
            vmem(blocks, width, LANES),
            vmem(blocks, width, FEATURES, dtype=half),
            vmem(blocks, width, LANES),
            vmem(blocks, SUBLANES, width),
        ),
        (tile_count, packed),
        [SMEM, VMEM],
        [rows, vmem(blocks, width, LANES), vmem(chunks, blocks * FEATURES, LANES), *factors, *bands, todo],
    )
    *k_in, tcol, lt, accl, accs = resident(*k_in, tcol, lt, accl, accs)
    k_out, image, even_out, odd_out, accl, listed = call(
        functools.partial(outer_kernel, reach),
        (
            vmem(reach * (reach + 1), width, width),
            vmem(blocks, width),
            shape(reach, width),
            shape(reach, width),
            vmem(blocks, width, LANES),
            vmem(SUBLANES, LANES),
        ),
        (tile_count, with_even, with_odd, packed, tcol, lt, accl, accs),
        [SMEM] + [VMEM] * 7,
        [rows, rows, *factors, *bands, todo],
        aliases={6: 4},
    )
    with_even, with_odd = swap(even_out, 0), swap(odd_out, 1)
    image, *k_in = resident(image, *k_in)
    accl, accs = call(
        functools.partial(again_kernel, reach),
        (vmem(blocks, width, LANES), vmem(blocks, SUBLANES, width)),
        (tile_count, image, *k_in),
        [SMEM] + [VMEM] * 4,
        [vmem(blocks, SUBLANES, width), vmem(blocks, width, LANES), vmem(chunks, LANES, LANES), todo],
    )
    k_out, accl, accs, listed = resident(k_out, accl, accs, listed)
    devices = lax.axis_size(AXES)
    again, sums, _ = call(
        functools.partial(close_kernel, reach),
        (vmem(blocks, width), shape(devices, LANES), vmem(blocks, width, LANES)),
        (tile_count, with_even, with_odd, listed, packed, image, k_out, accl, accs),
        [SMEM] + [VMEM] * 8,
        [vmem(2 * reach, SUBLANES, width), todo],
        aliases={7: 2},
    )
    sums = lax.all_to_all(sums, AXES, 0, 0, tiled=True)
    (again,) = resident(again)
    return call(
        finish_kernel,
        (shape(blocks, width), shape(blocks, width)),
        (sums, packed, image, again),
        [VMEM] * 4,
    )


def solution(mesh):
    in_specs = (
        P(("runs", "grp", "mem"), None, None),
        P(("runs", "grp", "mem"), None),
        P(("runs", "grp", "mem"), None),
        P(("runs", "grp", "mem"), None, None),
        P(("runs", "grp", "mem")),
    )
    out_specs = (P(("runs", "grp", "mem"), None), P(("runs", "grp", "mem"), None))
    return jax.shard_map(local, mesh=mesh, in_specs=in_specs, out_specs=out_specs, check_vma=False)
```

```python
import functools

import jax
import jax.numpy as jnp
from jax import lax
from jax.experimental import pallas as pl
from jax.experimental.pallas import tpu as pltpu
from jax.sharding import PartitionSpec as P

SCALE = 0.2 * 16.0
TINY = 1e-30
LANES = 128
SUBLANES = 8
BAND = 128
UNROLL = 16
AXES = ("grp", "mem")
MIB = 1 << 20
X, Y, T, V, N, COUNT, ODD = range(7)
NEAR = 4.0
PARTS = ((0, 0), (0, 1), (1, 0), (1, 1), (0, 2), (2, 0))
NORM = 2 * len(PARTS)
ONES, TIMES, VECTOR = NORM + 3, NORM + 6, NORM + 9
FEATURES = 32

VMEM = pl.BlockSpec(memory_space=pltpu.VMEM)
HBM = pl.BlockSpec(memory_space=pltpu.HBM)


def resident(*arrays):
    return [pltpu.with_memory_space_constraint(a, pltpu.VMEM) for a in arrays]


def call(kernel, out_shape, operands, specs, scratch=(), limit=8, aliases=None):
    return pl.pallas_call(
        kernel,
        out_shape=out_shape,
        in_specs=specs,
        out_specs=jax.tree.map(lambda _: VMEM, out_shape),
        scratch_shapes=list(scratch),
        input_output_aliases=aliases or {},
        compiler_params=pltpu.CompilerParams(vmem_limit_bytes=limit * MIB),
    )(*operands)


def shape(*dims):
    return jax.ShapeDtypeStruct(dims, jnp.float32)


def vmem(*dims, dtype=jnp.float32):
    return pltpu.VMEM(dims, dtype)


def entries(u, ti, tj, mode):
    s = u * lax.rsqrt(u)
    a = jnp.maximum(1.0 - s, 0.0)
    if mode == "same":
        d = jnp.abs(ti - tj)
        b = 1.0 - d
        f = d + 0.25
    else:
        b = jnp.maximum(ti - tj, 0.0)
        f = 1.25 - b
    p = a * b
    p = p * p
    return (p * p) * ((s + 0.25) * f)


def spread(row):
    return jnp.broadcast_to(row, (SUBLANES, row.shape[-1]))


def cut(ch):
    return slice(ch * LANES, (ch + 1) * LANES)


def block_at(c):
    return pl.ds(pl.multiple_of(c * SUBLANES, SUBLANES), SUBLANES)


def each_block(q, stride=SUBLANES):
    return pl.ds(q, SUBLANES, stride=stride)


def gather(rows, q):
    return jnp.concatenate([rows[ch, each_block(q), :] for ch in range(rows.shape[0])], axis=1)


def scatter(rows, at, z, first=0):
    for ch in range(z.shape[-1] // LANES):
        rows[first + ch, at, :] = z[:, cut(ch)]


def split(a):
    high = a.astype(jnp.bfloat16).astype(jnp.float32)
    rest = a - high
    middle = rest.astype(jnp.bfloat16).astype(jnp.float32)
    return [high, middle, rest - middle]


def left_features(x, y, t, v):
    xs, ys, one = split(x), split(y), jnp.ones_like(x)
    products = [xs[i] for i, _ in PARTS] + [ys[i] for i, _ in PARTS]
    return products + split(x * x + y * y) + [one] * 3 + split(t) + split(v)


def put_right(rt, wide, x, y):
    wide[...] = jnp.zeros_like(wide)
    xs, ys, one = split(x), split(y), jnp.ones_like(x)
    products = [-2.0 * xs[j] for _, j in PARTS] + [-2.0 * ys[j] for _, j in PARTS]
    for q, z in enumerate(products + [one] * 3 + split(x * x + y * y)):
        scatter(wide, each_block(q, FEATURES), z)
    for b in range(rt.shape[0]):
        for n in range(wide.shape[0]):
            rt[b, :, cut(n)] = wide[n, b * FEATURES : (b + 1) * FEATURES, :].astype(jnp.bfloat16)


def columns(lt, first, pairs):
    dims = (lt.shape[-1], LANES * pairs)
    row = lax.broadcasted_iota(jnp.int32, dims, 0) - first
    group = lax.broadcasted_iota(jnp.int32, dims, 1) // LANES
    pick = jnp.where((row >= 3 * group) & (row < 3 * group + 3), 1.0, 0.0)
    return jnp.dot(lt, pick.astype(jnp.bfloat16), preferred_element_type=jnp.float32)


def near(x, y):
    return jnp.max(jnp.maximum(jnp.abs(x), jnp.abs(y))) <= NEAR


def new_tile(fill, code, following, mode, diag, side, sign_of, k_ref, tcol, vcol, accl, accs, bufs):
    slot, r, c = code >> 8, (code >> 4) & 15, code & 15
    chunks = side.shape[0]
    bands = chunks * LANES // BAND
    sign = 1.0 if mode == "same" else sign_of(c)
    vj = [spread(side[ch, block_at(c), :][V : V + 1]) for ch in range(chunks)]
    tj = [sign * spread(side[ch, block_at(c), :][T : T + 1]) for ch in range(chunks)]
    zero = jnp.zeros((SUBLANES, LANES), jnp.float32)
    acc = [zero] * chunks
    for band in range(bands):
        first = band * BAND // LANES if diag else 0
        if band + 1 < bands:
            fill(bufs[(band + 1) % 2], r, c, band + 1, (band + 1) * BAND // LANES if diag else 0)
        else:
            fill(bufs[0], (following >> 4) & 15, following & 15, 0, 0)
        buf = bufs[band % 2]
        for g in range(BAND // SUBLANES):
            near_rows = slice(g * SUBLANES, (g + 1) * SUBLANES)
            at = slice(band * BAND + g * SUBLANES, band * BAND + (g + 1) * SUBLANES)
            ti = tcol[r, at, :]
            if mode == "next":
                ti = sign * ti + 1.0
            if accs is not None:
                vi = vcol[r, at, :]
            total = None
            for ch in range(first, chunks):
                m = entries(buf[near_rows, cut(ch)], ti, tj[ch], mode)
                k_ref[slot, at, cut(ch)] = m
                w = m * vj[ch]
                total = w if total is None else total + w
                if accs is not None and not (diag and ch == first):
                    acc[ch] = acc[ch] + m * vi
            accl[r, at, :] = total if diag else accl[r, at, :] + total
    if accs is not None:
        for ch in range(1 if diag else 0, chunks):
            accs[c, :, cut(ch)] += acc[ch]


def old_tile(code, row_of, k_ref, vcol, accl, accs, diag):
    slot, r, c = code >> 8, (code >> 4) & 15, code & 15
    width = k_ref.shape[-1]
    chunks = width // LANES
    vj = [spread(row_of(c, ch)) for ch in range(chunks)]
    zero = jnp.zeros((SUBLANES, LANES), jnp.float32)

    def rows_at(at, acc, used, single):
        acc = list(acc)
        if accs is not None:
            vi = vcol[r, at, :]
        total = None
        for q, ch in enumerate(used):
            m = k_ref[slot, at, cut(ch)]
            w = m * vj[ch]
            total = w if total is None else total + w
            if accs is not None and ch != single:
                acc[q] = acc[q] + m * vi
        accl[r, at, :] = total if diag else accl[r, at, :] + total
        return tuple(acc)

    def band(lo, hi, used, single):
        def step(it, acc):
            for g in range(UNROLL):
                start = pl.multiple_of((it * UNROLL + g) * SUBLANES, SUBLANES)
                acc = rows_at(pl.ds(start, SUBLANES), acc, used, single)
            return acc

        deep = SUBLANES * UNROLL
        acc = lax.fori_loop(lo // deep, hi // deep, step, tuple(zero for _ in used))
        if accs is not None:
            for q, ch in enumerate(used):
                if ch != single:
                    accs[c, :, cut(ch)] += acc[q]

    if diag:
        for ri in range(chunks):
            band(ri * LANES, (ri + 1) * LANES, list(range(ri, chunks)), ri)
    else:
        band(0, width, list(range(chunks)), -1)


def inner_slots(blocks, reach):
    return sum(blocks - k for k in range(reach + 1))


def with_counts(kernel):
    def run(reach, counts, *refs):
        *refs, held, sem = refs
        copy = pltpu.make_async_copy(counts.at[0:1, :], held, sem)
        copy.start()

        def ready():
            copy.wait()
            return lambda r: held[0, r]

        kernel(reach, ready, *refs)

    return run


def list_inner(blocks, reach, count, todo, same):
    for r in range(blocks):
        todo[r] = (r << 8) | (r << 4) | r
    at = jnp.int32(blocks)
    ends = [at]

    def put(at, r, k, base, keep):
        todo[at] = ((base + r) << 8) | (r << 4) | (r + k)
        return at + keep.astype(jnp.int32)

    def bit(r):
        return ((same >> r) & 1) == 1

    at = lax.fori_loop(0, blocks - 1, lambda r, at: put(at, r, 1, 0, (count(r) > 1) & bit(r)), at)
    ends.append(at)
    at = lax.fori_loop(0, blocks - 1, lambda r, at: put(at, r, 1, 0, (count(r) > 1) & ~bit(r)), at)
    ends.append(at)
    base = 0
    for k in range(2, reach + 1):
        at = lax.fori_loop(0, blocks - k, lambda r, at, k=k, base=base: put(at, r, k, base, count(r) > k), at)
        base += blocks - k
    todo[at] = 0
    return ends + [at]


def list_outer(blocks, reach, count, low_count, todo, same):
    tiles = []
    slot = 0
    for k in range(1, reach + 1):
        for j in range(k):
            c, r = reach - k + j, blocks - k + j
            tiles.append((k, 0, (slot << 8) | (j << 4) | c, ((low_count >> (3 * c)) & 7) > k))
            tiles.append((k, 1, ((slot + 1) << 8) | (r << 4) | (reach + j), count(r) > k))
            slot += 2
    at = jnp.int32(0)
    ends = []
    for wanted in (True, False):
        for k, which, code, keep in tiles:
            together = ((same >> which) & 1) == 1 if k == 1 else None
            if wanted and k > 1:
                continue
            if k == 1:
                keep = keep & (together if wanted else ~together)
            todo[at] = code
            at += keep.astype(jnp.int32)
        ends.append(at)
    todo[at] = 0
    return ends


def cell(rows, b):
    at = b * SUBLANES + T
    return jnp.floor(rows[0, at : at + 1, 0:1])


def as_scalar(value):
    return jnp.max(jnp.broadcast_to(value, (1, LANES))).astype(jnp.int32)


def flag(condition, weight):
    return jnp.where(condition, float(weight), 0.0)


def low_counts(low):
    total = jnp.zeros((1, 1), jnp.float32)
    for b in range(low.shape[1] // SUBLANES):
        at = b * SUBLANES + COUNT
        total += low[0, at : at + 1, 0:1] * float(8**b)
    return total


def pack_kernel(count_in, coords_in, vector_in, noise_in, even_out, odd_out, packed, counts, count, coords, vector, noise, sems):
    chunks = packed.shape[0]
    edge = even_out.shape[1]
    odd = lax.rem(position(), 2).astype(jnp.float32)
    copies = [
        pltpu.make_async_copy(source, target, sems.at[n])
        for n, (source, target) in enumerate(
            [(count_in, count), (coords_in, coords), (vector_in, vector), (noise_in, noise)]
        )
    ]
    for copy in copies:
        copy.start()
    for copy in copies:
        copy.wait()
    for q in (X, Y, T):
        scatter(packed, each_block(q), coords[q])
    scatter(packed, each_block(V), vector[...])
    scatter(packed, each_block(N), noise[...])
    lane = lax.broadcasted_iota(jnp.int32, (1, LANES), 1)
    row = jnp.zeros((1, LANES), jnp.int32)
    for b in range(vector.shape[0]):
        row = jnp.where(lane == b, count[b], row)
        at = b * SUBLANES + COUNT
        packed[:, at : at + 1, :] = jnp.full((chunks, 1, LANES), count[b].astype(jnp.float32))
        packed[:, at + 1 : (b + 1) * SUBLANES, :] = jnp.full((chunks, SUBLANES - ODD, LANES), odd)
    counts[...] = jnp.broadcast_to(row, counts.shape)
    first, last = packed[:, 0:edge, :], packed[:, packed.shape[1] - edge :, :]
    even_out[...], odd_out[...] = by_parity(packed, last, first)


def centre(packed):
    head = packed[0, 0:SUBLANES, :]
    mean = jnp.sum(head, axis=1, keepdims=True) * (1.0 / LANES)
    return mean[X : X + 1], mean[Y : Y + 1], cell(packed, 0)


def matmul_fill(lt, rt):
    def fill(buf, r, c, band, first):
        own = lt[r, band * BAND : (band + 1) * BAND, :]
        at = slice(first * LANES, buf.shape[-1])
        u = jnp.dot(own, rt[c, :, at], preferred_element_type=jnp.float32)
        buf[:, at] = jnp.maximum(u, TINY)

    return fill


def difference_fill(packed, raw):
    def fill(buf, r, c, band, first):
        own = packed[band * BAND // LANES, block_at(r), :].T
        for ch in range(first, raw.shape[0]):
            other = raw[ch, block_at(c), :]
            dx, dy = [own[:, q : q + 1] - other[q : q + 1, :] for q in (X, Y)]
            buf[:, cut(ch)] = jnp.maximum(dx * dx + dy * dy, TINY)

    return fill


def run_tiles(fill, todo, ends, modes, tile):
    code = todo[0]
    fill((code >> 4) & 15, code & 15)
    begin = 0
    for end, mode in zip(ends, modes):

        def body(n, _, mode=mode):
            tile(todo[n], todo[n + 1], mode)
            return 0

        lax.fori_loop(begin, end, body, 0)
        begin = end


def inner_kernel(
    reach, ready, packed, k_same, k_next, k_far, tcol, lt, accl, accs, rows, vcol, flat, wide, rt, buf_a, buf_b, todo
):
    blocks = accs.shape[0]
    cx, cy, start = centre(packed)
    x, y = gather(packed, X) - cx, gather(packed, Y) - cy
    t, v = gather(packed, T) - start, gather(packed, V)
    flat[...] = jnp.zeros_like(flat)
    for q, z in enumerate(left_features(x, y, t, v)):
        scatter(flat, each_block(q, FEATURES), z)
    put_right(rt, wide, x, y)
    scatter(rows, each_block(T), t)
    scatter(rows, each_block(V), v)
    for b in range(blocks):
        for ch in range(flat.shape[0]):
            part = flat[ch, b * FEATURES : (b + 1) * FEATURES, :].T
            lt[b, cut(ch), :] = part.astype(jnp.bfloat16)
        both = columns(lt[b], TIMES, 2)
        tcol[b] = both[:, :LANES]
        vcol[b] = both[:, LANES:]
    accs[...] = jnp.zeros_like(accs)
    same = jnp.zeros((1, 1), jnp.float32)
    for r in range(blocks - 1):
        same += flag(cell(packed, r) == cell(packed, r + 1), 1 << r)
    ends = list_inner(blocks, reach, ready(), todo, as_scalar(same))
    bufs = (buf_a, buf_b)
    kinds = (("same", k_same), ("same", k_next), ("next", k_next), ("next", k_far))

    def run(fill):
        def tile(code, following, kind):
            mode, k_ref = kind
            new_tile(
                fill, code, following, mode, k_ref is k_same,
                rows, lambda c: 1.0, k_ref, tcol, vcol, accl, accs, bufs,
            )

        run_tiles(lambda r, c: fill(buf_a, r, c, 0, 0), todo, ends, kinds, tile)

    fast = near(x, y)
    pl.when(fast)(lambda: run(matmul_fill(lt, rt)))
    pl.when(jnp.logical_not(fast))(lambda: run(difference_fill(packed, packed)))


def outer_kernel(
    reach, ready, with_even, with_odd, packed, tcol, lt, accl_in, accs,
    k_ref, image, even_out, odd_out, accl, listed, raw, rows, wide, rt, buf_a, buf_b, todo,
):
    blocks = accs.shape[0]
    edge = reach * SUBLANES
    cx, cy, start = centre(packed)
    raw[...] = jnp.zeros_like(raw)
    high, low = by_parity(packed, with_even[...], with_odd[...])
    raw[:, 0:edge, :] = low
    raw[:, edge : 2 * edge, :] = high
    x, y = gather(raw, X) - cx, gather(raw, Y) - cy
    t = gather(raw, T) - start
    place = lax.broadcasted_iota(jnp.int32, (SUBLANES, 1), 0)
    put_right(rt, wide, x, y)
    scatter(rows, each_block(T), t)
    scatter(rows, each_block(V), gather(raw, V))
    scalars = low_counts(low)
    listed[...] = jnp.broadcast_to(scalars, listed.shape)
    scalars += flag(cell(low, reach - 1) == cell(packed, 0), 1 << (3 * reach))
    scalars += flag(cell(packed, blocks - 1) == cell(high, 0), 1 << (3 * reach + 1))
    code = as_scalar(scalars)
    ends = list_outer(blocks, reach, ready(), code, todo, code >> (3 * reach))
    bufs = (buf_a, buf_b)

    def run(fill):
        def tile(code, following, mode):
            new_tile(
                fill, code, following, mode, False,
                rows, lambda c: jnp.where(c < reach, -1.0, 1.0), k_ref, tcol, None, accl, None, bufs,
            )

        run_tiles(lambda r, c: fill(buf_a, r, c, 0, 0), todo, ends, ("same", "next"), tile)

    halo = jnp.where(place < 2 * reach, 1.0, 0.0)
    own_x, own_y = gather(packed, X) - cx, gather(packed, Y) - cy
    reach_x = jnp.maximum(jnp.abs(x * halo), jnp.abs(own_x))
    reach_y = jnp.maximum(jnp.abs(y * halo), jnp.abs(own_y))
    fast = near(reach_x, reach_y)
    pl.when(fast)(lambda: run(matmul_fill(lt, rt)))
    pl.when(jnp.logical_not(fast))(lambda: run(difference_fill(packed, raw)))
    summed = jnp.sum(accs[...], axis=1) + jnp.sum(accl[...], axis=-1)
    image[...] = gather(packed, N) * gather(packed, V) + SCALE * summed
    even_out[...], odd_out[...] = by_parity(packed, image[blocks - reach :, :], image[0:reach, :])


def again_kernel(reach, ready, image, k_same, k_next, k_far, accl, accs, rows, vcol, flat, todo):
    blocks, width = image.shape
    flat[...] = jnp.zeros_like(flat)
    for n, part in enumerate(split(image[...])):
        scatter(flat, pl.ds(n, blocks, stride=3), part)
    lt = jnp.concatenate([flat[ch].T for ch in range(flat.shape[0])], axis=0).astype(jnp.bfloat16)
    for b in range(blocks):
        rows[b, 0:1, :] = image[b : b + 1, :]
    for b in range(0, blocks, 2):
        both = columns(lt, 3 * b, 2)
        vcol[b] = both[:, :LANES]
        vcol[b + 1] = both[:, LANES:]
    accs[...] = jnp.zeros_like(accs)
    ends = list_inner(blocks, reach, ready(), todo, jnp.int32(0))

    def row_of(c, ch):
        return rows[c, 0:1, cut(ch)]

    for begin, end, k_ref in ((0, ends[0], k_same), (ends[0], ends[2], k_next), (ends[2], ends[3], k_far)):

        def body(n, _, k_ref=k_ref):
            old_tile(todo[n], row_of, k_ref, vcol, accl, accs, k_ref is k_same)
            return 0

        lax.fori_loop(begin, end, body, 0)


def dots(pairs):
    lane = lax.broadcasted_iota(jnp.int32, (1, LANES), 1)
    out = jnp.zeros((1, LANES), jnp.float32)
    for n, (a, b) in enumerate(pairs):
        total = jnp.sum(jnp.sum(a * b, axis=1, keepdims=True), axis=0, keepdims=True)
        out = jnp.where(lane == n, total, out)
    return out


def close_kernel(
    reach, ready, with_even, with_odd, listed, packed, image, k_ref, accl_in, accs, again, sums, accl, rows, todo
):
    blocks = image.shape[0]
    high, low = by_parity(packed, with_even[...], with_odd[...])
    for b in range(reach):
        rows[b, 0:1, :] = low[b : b + 1, :]
        rows[reach + b, 0:1, :] = high[b : b + 1, :]
    ends = list_outer(blocks, reach, ready(), as_scalar(listed[0:1, :]), todo, jnp.int32(0))

    def body(n, _):
        old_tile(todo[n], lambda c, ch: rows[c, 0:1, cut(ch)], k_ref, None, accl, None, False)
        return 0

    lax.fori_loop(0, ends[-1], body, 0)
    summed = jnp.sum(accs[...], axis=1) + jnp.sum(accl[...], axis=-1)
    q = image[...]
    p = gather(packed, N) * q + SCALE * summed
    again[...] = p
    b = gather(packed, V)
    sums[...] = jnp.broadcast_to(dots([(b, b), (b, q), (q, q), (b, p), (q, p)]), sums.shape)


def finish_kernel(sums, packed, image, again, solution, residual):
    total = jnp.sum(sums[...], axis=0, keepdims=True)
    bb, bq, qq, bp, qp = [total[:, n : n + 1] for n in range(5)]
    alpha = bb / bq
    rq = bq - alpha * qq
    rr = (bb - alpha * bq) - alpha * rq
    beta = rr / bb
    r_ar = rq - alpha * (bp - alpha * qp)
    b_ar = bq - alpha * bp
    curvature = r_ar + beta * (rq + b_ar) + beta * beta * bq
    gamma = rr / curvature
    b, q, p = gather(packed, V), image[...], again[...]
    r = b - alpha * q
    d = r + beta * b
    ad = (q - alpha * p) + beta * q
    solution[...] = alpha * b + gamma * d
    residual[...] = r - gamma * ad


def position():
    place = 0
    for axis in AXES:
        place = place * lax.axis_size(axis) + lax.axis_index(axis)
    return place


def by_parity(packed, low, high):
    odd = packed[0, ODD : ODD + 1, 0:1] > 0.5
    return jnp.where(odd, high, low), jnp.where(odd, low, high)


def swap(value, start):
    pairs = [(i, i + 1) for i in range(start, lax.axis_size(AXES) - 1, 2)]
    return lax.ppermute(value, AXES, pairs + [(b, a) for a, b in pairs])


def local(coords, noise, right_side, tiles, tile_count):
    blocks, width = right_side.shape
    reach = tiles.shape[1] - 1
    chunks = width // LANES
    edge = (chunks, reach * SUBLANES, LANES)
    half = jnp.bfloat16
    inner = inner_slots(blocks, reach) - blocks
    bands = [vmem(BAND, width), vmem(BAND, width)]
    factors = [vmem(chunks, SUBLANES * FEATURES, LANES), vmem(SUBLANES, FEATURES, width, dtype=half)]
    rows = vmem(chunks, SUBLANES * SUBLANES, LANES)
    todo = pltpu.SMEM((inner + blocks + 2,), jnp.int32)
    held = [pltpu.SMEM((1, LANES), jnp.int32), pltpu.SemaphoreType.DMA]

    operands = (tile_count, jnp.transpose(coords, (1, 0, 2)), right_side, noise)
    even_out, odd_out, packed, counts = call(
        pack_kernel,
        (shape(*edge), shape(*edge), vmem(chunks, blocks * SUBLANES, LANES), vmem(SUBLANES, LANES, dtype=jnp.int32)),
        [pltpu.with_memory_space_constraint(a, pltpu.HBM) for a in operands],
        [HBM] * 4,
        [
            pltpu.SMEM((blocks,), jnp.int32),
            vmem(3, blocks, width),
            vmem(blocks, width),
            vmem(blocks, width),
            pltpu.SemaphoreType.DMA((4,)),
        ],
    )
    with_even, with_odd = swap(even_out, 0), swap(odd_out, 1)
    packed, counts = resident(packed, counts)
    *k_in, tcol, lt, accl, accs = call(
        functools.partial(with_counts(inner_kernel), reach),
        (
            vmem(blocks, width, width),
            vmem(blocks - 1, width, width),
            vmem(inner - blocks + 1, width, width),
            vmem(blocks, width, LANES),
            vmem(blocks, width, FEATURES, dtype=half),
            vmem(blocks, width, LANES),
            vmem(blocks, SUBLANES, width),
        ),
        (counts, packed),
        [VMEM] * 2,
        [rows, vmem(blocks, width, LANES), vmem(chunks, blocks * FEATURES, LANES), *factors, *bands, todo, *held],
    )
    *k_in, tcol, lt, accl, accs = resident(*k_in, tcol, lt, accl, accs)
    k_out, image, even_out, odd_out, accl, listed = call(
        functools.partial(with_counts(outer_kernel), reach),
        (
            vmem(reach * (reach + 1), width, width),
            vmem(blocks, width),
            shape(reach, width),
            shape(reach, width),
            vmem(blocks, width, LANES),
            vmem(SUBLANES, LANES),
        ),
        (counts, with_even, with_odd, packed, tcol, lt, accl, accs),
        [VMEM] * 8,
        [rows, rows, *factors, *bands, todo, *held],
        aliases={6: 4},
    )
    with_even, with_odd = swap(even_out, 0), swap(odd_out, 1)
    image, *k_in = resident(image, *k_in)
    accl, accs = call(
        functools.partial(with_counts(again_kernel), reach),
        (vmem(blocks, width, LANES), vmem(blocks, SUBLANES, width)),
        (counts, image, *k_in),
        [VMEM] * 5,
        [vmem(blocks, SUBLANES, width), vmem(blocks, width, LANES), vmem(chunks, LANES, LANES), todo, *held],
    )
    k_out, accl, accs, listed = resident(k_out, accl, accs, listed)
    devices = lax.axis_size(AXES)
    again, sums, _ = call(
        functools.partial(with_counts(close_kernel), reach),
        (vmem(blocks, width), shape(devices, LANES), vmem(blocks, width, LANES)),
        (counts, with_even, with_odd, listed, packed, image, k_out, accl, accs),
        [VMEM] * 9,
        [vmem(2 * reach, SUBLANES, width), todo, *held],
        aliases={7: 2},
    )
    sums = lax.all_to_all(sums, AXES, 0, 0, tiled=True)
    (again,) = resident(again)
    return call(
        finish_kernel,
        (shape(blocks, width), shape(blocks, width)),
        (sums, packed, image, again),
        [VMEM] * 4,
    )


def solution(mesh):
    in_specs = (
        P(("runs", "grp", "mem"), None, None),
        P(("runs", "grp", "mem"), None),
        P(("runs", "grp", "mem"), None),
        P(("runs", "grp", "mem"), None, None),
        P(("runs", "grp", "mem")),
    )
    out_specs = (P(("runs", "grp", "mem"), None), P(("runs", "grp", "mem"), None))
    return jax.shard_map(local, mesh=mesh, in_specs=in_specs, out_specs=out_specs, check_vma=False)
```
